256 devices in a mesh: row: 8 (over y, z_hi), col: 32 (over x, z_lo, core).
Axes of the slice: x: 4, y: 4, z: 8 (z_hi: 2, z_lo: 4; z = z_hi * 4 + z_lo), core: 2. Of those that a mesh axis runs over, the one named last changes fastest.
Arguments:
- query: bfloat16 [32768, 256], P(('row', 'col')), may hold values from -30 to 30
- key: bfloat16 [32768, 128], P(('row', 'col')), may hold values from -6 to 6
- value: bfloat16 [32768, 128], P(('row', 'col')), may hold values from -6 to 6
- out_grad: bfloat16 [32768, 256], P(('row', 'col')), may hold values from -6 to 6
- attn_out: bfloat16 [32768, 256], P(('row', 'col')), may hold values from -6 to 6
- lse: float32 [32768, 2], P(('row', 'col')), may hold values from -40 to 400, as said below
- positions: int32 [32768], replicated, may hold values from 0 to 32767, as said below
Outputs:
- query_grad: bfloat16 [32768, 256], P(('row', 'col'))
- key_grad: bfloat16 [32768, 128], P(('row', 'col'))
- value_grad: bfloat16 [32768, 128], P(('row', 'col'))
The draws below stay inside these ranges and needn't reach their ends.
Inputs may be any that keep to these rules, and one draw needn't show every extreme that they name: A permutation of 0 to 32767; each aligned run of 64 stored rows holds 64 consecutive positions in rising order. `lse`: the forward pass's log of the sum over allowed keys of exp(scores) for each row and query head.
All inputs are finite; a program needn't handle non-finite values.
Results may differ from the reference program's by a relative error of at most 0.011.
Values may be sent and summed in bfloat16 or wider, within the bound.
A program may use at most 64 MiB of HBM per device.

```python
import math
import jax
import jax.numpy as jnp
from jax import lax

HEAD_DIM = 128
GROUP = 2
KV_HEADS = 1
BLOCK = 64
TOKENS = 32768


def draw_query(key, part):
    key = jax.random.fold_in(key, 3)
    values = jax.random.truncated_normal(key, -6.0, 6.0, (TOKENS, KV_HEADS, GROUP, HEAD_DIM), jnp.float32)
    return values.reshape(TOKENS, KV_HEADS * GROUP * HEAD_DIM).astype(jnp.bfloat16)


def draw_key(key, part):
    key = jax.random.fold_in(key, 5)
    values = jax.random.truncated_normal(key, -6.0, 6.0, (TOKENS, KV_HEADS, HEAD_DIM), jnp.float32)
    return values.reshape(TOKENS, KV_HEADS * HEAD_DIM).astype(jnp.bfloat16)


def draw_positions(key, part):
    key = jax.random.fold_in(key, 7)
    order = jax.random.permutation(key, TOKENS // BLOCK)
    spread = order[:, None] * BLOCK + jnp.arange(BLOCK)[None, :]
    return spread.reshape(TOKENS).astype(jnp.int32)


def draw_lse(key, part):
    queries = draw_query(key, part).astype(jnp.float32).reshape(TOKENS, KV_HEADS, GROUP, HEAD_DIM)
    keys = draw_key(key, part).astype(jnp.float32).reshape(TOKENS, KV_HEADS, HEAD_DIM)
    places = draw_positions(key, part)
    block = math.gcd(TOKENS, 512)
    count = TOKENS // block
    scale = 1.0 / math.sqrt(HEAD_DIM)

    def per_block(pieces):
        q_block, pos_block = pieces
        allowed = places[None, :] <= pos_block[:, None]
        scores = jnp.einsum('qgcd,kgd->qgck', q_block, keys, precision=lax.Precision.HIGHEST) * scale
        scores = jnp.where(allowed[:, None, None, :], scores, -1e+30)
        peak = jnp.max(scores, -1)
        total = jnp.sum(jnp.where(allowed[:, None, None, :], jnp.exp(scores - peak[..., None]), 0.0), -1)
        return peak + jnp.log(total)
    result = lax.map(per_block, (queries.reshape(count, block, KV_HEADS, GROUP, HEAD_DIM), places.reshape(count, block)))
    return result.reshape(TOKENS, KV_HEADS * GROUP).astype(jnp.float32)


def level_of(rng, shape, cuts, smallest, top_value):
    loudness = 1.0
    for axis_at, shards_of in cuts:
        draws = jax.random.uniform(jax.random.fold_in(jax.random.fold_in(rng, 6), axis_at), (shards_of,), jnp.float32, smallest / len(cuts), top_value / len(cuts))
        loudness = loudness * jnp.repeat(jnp.exp(draws), shape[axis_at] // shards_of).reshape((-1,) + (1,) * (len(shape) - 1 - axis_at))
    return loudness


def bell_draw(stream_key, shape, scale, reach, split=(), held_as=jnp.bfloat16):
    values = scale * jax.random.normal(stream_key, shape, jnp.float32)
    if split:
        values = values * level_of(stream_key, shape, split, -0.22, 0.18)
    return jnp.clip(values, -reach, reach).astype(held_as)


def setup_inputs(seed: int = 0) -> dict:
    key_of = jax.random.split(jax.random.key(seed), 8)
    return {
        "query": draw_query(jax.random.fold_in(key_of[7], 71), 0),
        "key": draw_key(jax.random.fold_in(key_of[7], 71), 0),
        "value": bell_draw(key_of[2], (TOKENS, KV_HEADS * HEAD_DIM), 1.0, 6.0, ((0, 256),)),
        "out_grad": bell_draw(key_of[3], (TOKENS, KV_HEADS * GROUP * HEAD_DIM), 1.0, 6.0, ((0, 256),)),
        "attn_out": bell_draw(key_of[4], (TOKENS, KV_HEADS * GROUP * HEAD_DIM), 1.0, 6.0, ((0, 256),)),
        "lse": draw_lse(jax.random.fold_in(key_of[7], 71), 0),
        "positions": draw_positions(jax.random.fold_in(key_of[7], 71), 0),
    }


NEG = -1e+30

def reference(query, key, value, out_grad, attn_out, lse, positions):
    scale = 1.0 / math.sqrt(HEAD_DIM)
    block = math.gcd(TOKENS, 512)
    count = TOKENS // block
    q_all = query.reshape(count, block, KV_HEADS, GROUP, HEAD_DIM)
    do_all = out_grad.reshape(count, block, KV_HEADS, GROUP, HEAD_DIM)
    o_all = attn_out.reshape(count, block, KV_HEADS, GROUP, HEAD_DIM)
    lse_all = lse.reshape(count, block, KV_HEADS, GROUP)
    pos_all = positions.reshape(count, block)
    keys = key.reshape(TOKENS, KV_HEADS, HEAD_DIM).astype(jnp.float32)
    values = value.reshape(TOKENS, KV_HEADS, HEAD_DIM).astype(jnp.float32)

    def step(carry, pieces):
        key_acc, value_acc = carry
        q_block, do_block, o_block, lse_rows, pos_block = pieces
        q_wide = q_block.astype(jnp.float32)
        do_wide = do_block.astype(jnp.float32)
        allowed = positions[None, :] <= pos_block[:, None]
        scores = jnp.einsum('qgcd,kgd->gcqk', q_wide, keys) * scale
        lse_block = jnp.transpose(lse_rows, (1, 2, 0))
        probs = jnp.where(allowed[None, None], jnp.exp(scores - lse_block[..., None]), 0.0)
        delta = jnp.transpose(lax.optimization_barrier(jnp.sum(do_wide * o_block.astype(jnp.float32), -1)), (1, 2, 0))
        dprobs = jnp.einsum('qgcd,kgd->gcqk', do_wide, values)
        dscores = (probs * (dprobs - delta[..., None])).astype(jnp.bfloat16).astype(jnp.float32)
        probs_low = probs.astype(jnp.bfloat16).astype(jnp.float32)
        q_grad = jnp.einsum('gcqk,kgd->qgcd', dscores, keys) * scale
        key_acc = key_acc + jnp.einsum('gcqk,qgcd->kgd', dscores, q_wide)
        value_acc = value_acc + jnp.einsum('gcqk,qgcd->kgd', probs_low, do_wide)
        return ((key_acc, value_acc), q_grad.astype(jnp.bfloat16))
    zeros = jnp.zeros((TOKENS, KV_HEADS, HEAD_DIM), jnp.float32)
    (key_acc, value_acc), q_grads = lax.scan(step, (zeros, zeros), (q_all, do_all, o_all, lse_all, pos_all))
    query_grad = q_grads.reshape(TOKENS, KV_HEADS * GROUP * HEAD_DIM)
    key_grad = (key_acc * scale).astype(jnp.bfloat16).reshape(TOKENS, KV_HEADS * HEAD_DIM)
    value_grad = value_acc.astype(jnp.bfloat16).reshape(TOKENS, KV_HEADS * HEAD_DIM)
    return (query_grad, key_grad, value_grad)
```

```python
import functools
import math

import jax
import jax.numpy as jnp
from jax import lax
from jax.experimental import pallas as pl
from jax.experimental.pallas import tpu as pltpu
from jax.sharding import PartitionSpec as P

F32 = jnp.float32
BF16 = jnp.bfloat16
MESH = pl.DeviceIdType.MESH
ROWS = 128
DIM = 128
NX, NY, NZ = 4, 4, 8
AUG = 16
REST = 112
SCALE = 1.0 / math.sqrt(DIM)
EXP_SCALE = math.log2(math.e) / math.sqrt(DIM)
FAR = -1e30
NT = (((1,), (1,)), ((), ()))

TILES = (
    (0, 0), (0, 1), (0, 3), (3, 1), (3, 3), (1, 1), (1, 3), (2, 1),
    (2, 3), (2, 2), (2, 0), (1, 2), (1, 0), (0, 2), (3, 2), (3, 0),
)


def table(values):
    total = 0
    for at, value in enumerate(values):
        total += value * 4**at
    return total


def place():
    row, col = lax.axis_index("row"), lax.axis_index("col")
    x, z_lo, core = col // 8, (col // 2) % 4, col % 2
    y, z_hi = row // 2, row % 2
    return x, y, z_hi * 4 + z_lo, core


def device(x, y, z, core):
    return (y * 2 + z // 4, x * 8 + (z % 4) * 2 + core)


def kernel(
    query, key, value, out_grad, attn_out, lse, positions,
    query_grad, key_grad, value_grad,
    qd, qm, kv, kt, ka, kp, dq, dk, dv,
    sib_out, sib_in, dq_out, dq_in, dkv_out, dkv_in,
    kv_send, kv_recv, ring_send, q_recv, pair_send,
    sib_send, sib_recv, dq_send, dq_recv, dkv_send, dkv_recv,
):
    x, y, z, core = place()
    other = 1 - core

    def plane(ox, oy):
        return device((x + ox) % NX, (y + oy) % NY, z, core)

    def along(oz, which=None):
        return device(x, y, (z + oz) % NZ, core if which is None else which)

    sibling = device(x, y, z, other)
    plane_offsets = [(ox, oy) for oy in (0, 1, 3, 2) for ox in (1, 3, 2, 0) if ox or oy]

    barrier = pltpu.get_barrier_semaphore()
    peers = [plane(ox, oy) for ox, oy in plane_offsets]
    peers += [along(oz) for oz in range(1, NZ)] + [sibling]
    for peer in peers:
        pl.semaphore_signal(barrier, inc=1, device_id=peer, device_id_type=MESH)

    kv[0, 0] = key[...]
    kv[0, 1] = value[...]
    line = lax.broadcasted_iota(jnp.int32, (AUG, ROWS), 0)

    def split_rows(term):
        high = term.astype(BF16).astype(F32)
        rest = term - high
        middle = rest.astype(BF16).astype(F32)
        low = rest - middle
        picked = jnp.where(line == 0, high, jnp.where(line == 1, middle, low))
        return jnp.where(line < 3, picked, 0.0).astype(BF16)

    for head in range(2):
        cut = pl.ds(head * DIM, DIM)
        grads, outs = out_grad[:, cut], attn_out[:, cut]
        delta = jnp.sum((grads.astype(F32) * outs.astype(F32)).T, axis=0, keepdims=True)
        wide = jnp.broadcast_to(lse[:, head : head + 1], (ROWS, ROWS)).T
        qd[0, head, 0:DIM] = query[:, cut].T
        qd[0, head, DIM : DIM + AUG] = split_rows(wide[0:1] * -math.sqrt(DIM))
        qd[0, 2 + head, 0:DIM] = grads.T
        qd[0, 2 + head, DIM : DIM + AUG] = split_rows(-delta)

    pl.semaphore_wait(barrier, len(peers))

    def ring_copy(source, target, part, at, oz):
        return pltpu.make_async_remote_copy(
            src_ref=qd.at[source] if part is None else qd.at[source, pl.ds(part * 2, 2)],
            dst_ref=qd.at[target] if part is None else qd.at[target, pl.ds(part * 2, 2)],
            send_sem=ring_send.at[at],
            recv_sem=q_recv.at[16 if part else target],
            device_id=along(oz),
            device_id_type=MESH,
        )

    def pair_copy(oz):
        return pltpu.make_async_remote_copy(
            src_ref=qd.at[2 * oz],
            dst_ref=qd.at[2 * oz + 1],
            send_sem=pair_send.at[oz],
            recv_sem=q_recv.at[2 * oz + 1],
            device_id=sibling,
            device_id_type=MESH,
        )

    rights = [ring_copy(0, 14, None, 0, 1), ring_copy(14, 12, None, 1, 1),
              ring_copy(12, 10, None, 2, 1), ring_copy(10, 8, 0, 3, 1)]
    lefts = [ring_copy(0, 2, None, 4, -1 + NZ), ring_copy(2, 4, None, 5, -1 + NZ),
             ring_copy(4, 6, None, 6, -1 + NZ), ring_copy(6, 8, 1, 7, -1 + NZ)]
    pairs = [pair_copy(oz) for oz in range(NZ)]

    def kv_copy(ox, oy):
        there = (NY - oy) % NY * 4 + (NX - ox) % NX
        return pltpu.make_async_remote_copy(
            src_ref=kv.at[0],
            dst_ref=kv.at[there],
            send_sem=kv_send.at[oy * 4 + ox],
            recv_sem=kv_recv.at[there],
            device_id=plane(ox, oy),
            device_id_type=MESH,
        )

    kv_copies = {offset: kv_copy(*offset) for offset in plane_offsets}

    rights[0].start()
    lefts[0].start()
    for offset in plane_offsets:
        kv_copies[offset].start()
    pairs[0].start()

    dq[...] = jnp.zeros_like(dq)
    dk[...] = jnp.zeros_like(dk)
    dv[...] = jnp.zeros_like(dv)
    lane = lax.broadcasted_iota(jnp.int32, (ROWS, ROWS), 1)
    block = lax.broadcasted_iota(jnp.int32, (ROWS, ROWS), 0) // 64
    for slot in range(16):
        hot = (lane < 3) | (lane == AUG + 2 * slot + block)
        ka[slot] = jnp.where(hot, 1.0, 0.0).astype(BF16)
        r, c = plane(slot % 4, slot // 4)
        places = positions[pl.ds(r * 32 + c, 1), :] // 64
        kp[2 * slot : 2 * slot + 1, :] = jnp.broadcast_to(places[:, 0:1], (1, ROWS))
        kp[2 * slot + 1 : 2 * slot + 2, :] = jnp.broadcast_to(places[:, 64:65], (1, ROWS))
    for slot in range(16):
        r, c = along(slot // 2, other if slot % 2 else core)
        places = positions[pl.ds(r * 32 + c, 1), :] // 64
        bias = jnp.where(kp[...] < places, 0.0, FAR)
        qm[slot] = jnp.concatenate([bias, jnp.zeros((REST - 32, ROWS), F32)], 0).astype(BF16)

    none = jnp.zeros((REST, ROWS), BF16)

    def turn(slot):
        kt[slot] = kv[slot, 0].T

    turn(0)
    keys = jnp.concatenate([kv[0, 0], ka[0]], 1)
    values = jnp.concatenate([kv[0, 1], ka[0]], 1)
    q_own = [qd[0, head] for head in range(4)]
    q_cat = jnp.concatenate([jnp.concatenate([part, none], 0) for part in q_own[:2]], 1)
    d_cat = jnp.concatenate([jnp.concatenate([part, none], 0) for part in q_own[2:]], 1)
    scores = jnp.dot(keys, q_cat, preferred_element_type=F32)
    dprobs = jnp.dot(values, d_cat, preferred_element_type=F32)
    at_key = lax.broadcasted_iota(jnp.int32, (ROWS, 2 * ROWS), 0)
    at_row = lax.broadcasted_iota(jnp.int32, (ROWS, 2 * ROWS), 1) % ROWS
    inside = (at_key <= at_row) & (at_key // 64 == at_row // 64)
    probs = jnp.where(inside, jnp.exp2(scores * EXP_SCALE), 0.0)
    dscores = (probs * dprobs).astype(BF16)
    dv[0] = lax.dot_general(d_cat[:DIM], probs.astype(BF16), NT, preferred_element_type=F32)
    dk[0] = lax.dot_general(q_cat[:DIM], dscores, NT, preferred_element_type=F32)
    part = jnp.dot(kt[0], dscores, preferred_element_type=F32)
    dq[0] = jnp.concatenate([part[:, :ROWS], part[:, ROWS:]], 0)

    def wait_keys(group):
        for ox in range(NX):
            if ox or group:
                offset = ((NX - ox) % NX, (NY - group) % NY)
                kv_copies[offset].wait_recv()
                turn(group * 4 + ox)

    def dkv_copy(ox, oy):
        there = (NY - oy) % NY * 4 + (NX - ox) % NX
        return pltpu.make_async_remote_copy(
            src_ref=dkv_out.at[oy * 4 + ox],
            dst_ref=dkv_in.at[there],
            send_sem=dkv_send.at[oy * 4 + ox],
            recv_sem=dkv_recv.at[there],
            device_id=plane(ox, oy),
            device_id_type=MESH,
        )

    dkv_copies = {offset: dkv_copy(*offset) for offset in plane_offsets}

    def send_keys(group):
        for ox in (2, 1, 3, 0):
            if ox or group:
                slot = group * 4 + ox
                dkv_out[slot, 0:DIM] = dk[slot].astype(BF16)
                dkv_out[slot, DIM:] = dv[slot].astype(BF16)
                dkv_copies[(ox, group)].start()

    def sib_copy(oz):
        return pltpu.make_async_remote_copy(
            src_ref=sib_out.at[oz],
            dst_ref=sib_in.at[oz],
            send_sem=sib_send.at[oz],
            recv_sem=sib_recv.at[oz],
            device_id=sibling,
            device_id_type=MESH,
        )

    sib_copies = [sib_copy(oz) for oz in range(NZ)]

    def dq_copy(oz):
        return pltpu.make_async_remote_copy(
            src_ref=dq_out.at[oz],
            dst_ref=dq_in.at[NZ - oz],
            send_sem=dq_send.at[oz],
            recv_sem=dq_recv.at[NZ - oz],
            device_id=along(oz),
            device_id_type=MESH,
        )

    dq_copies = {oz: dq_copy(oz) for oz in range(1, NZ)}

    def swap_queries(group):
        for oz in (2 * group, 2 * group + 1):
            sib_out[oz] = dq[2 * oz + 1].astype(BF16)
            sib_copies[oz].start()

    def send_queries(group):
        for oz in (2 * group, 2 * group + 1):
            sib_copies[oz].wait_recv()
            total = dq[2 * oz] + sib_in[oz].astype(F32)
            if oz:
                dq_out[oz] = total.astype(BF16)
                dq_copies[oz].start()
            else:
                dq[0] = total

    def hop(step):
        rights[step - 1].wait_recv()
        rights[step].start()
        lefts[step - 1].wait_recv()
        lefts[step].start()
        pairs[NZ - step].start()
        pairs[step].start()

    def before(step):
        if step == 0:
            hop(1)
            wait_keys(0)
            pairs[0].wait_recv()
            pairs[1].wait_recv()
        if step == 1:
            wait_keys(1)
        if step == 2:
            hop(2)
            wait_keys(3)
        if step == 3:
            pairs[7].wait_recv()
            pairs[6].wait_recv()
        if step == 4:
            hop(3)
        if step == 5:
            pairs[2].wait_recv()
            pairs[3].wait_recv()
            wait_keys(2)
        if step == 6:
            rights[3].wait_recv()
            lefts[3].wait_recv()
            pairs[4].start()
        if step == 7:
            pairs[4].wait_recv()
            pairs[5].wait_recv()

    def after(step):
        if step == 7:
            send_keys(1)
        if step == 8:
            send_keys(3)
        if step == 10:
            swap_queries(2)
        if step == 11:
            send_queries(2)
        if step == 12:
            swap_queries(1)
        if step == 13:
            send_queries(1)
            swap_queries(0)
        if step == 14:
            send_keys(2)
            send_queries(0)
        if step == 15:
            swap_queries(3)
            send_keys(0)
            send_queries(3)

    def tile(at_q, at_k):
        first_q, first_k = at_q * 4, at_k * 4
        marks = ka[pl.ds(first_k, 4)].reshape(4 * ROWS, ROWS)
        k_part = kv[pl.ds(first_k, 4), 0].reshape(4 * ROWS, DIM)
        v_part = kv[pl.ds(first_k, 4), 1].reshape(4 * ROWS, DIM)
        k_wide = jnp.concatenate([k_part, marks], 1)
        v_wide = jnp.concatenate([v_part, marks], 1)
        q_cols = [
            jnp.concatenate([qd[first_q + a, head], qm[first_q + a]], 0)
            for a in range(4)
            for head in range(2)
        ]
        d_cols = [
            jnp.concatenate([qd[first_q + a, 2 + head], none], 0)
            for a in range(4)
            for head in range(2)
        ]
        q_wide = jnp.concatenate(q_cols, 1)
        d_wide = jnp.concatenate(d_cols, 1)
        scores = jnp.dot(k_wide, q_wide, preferred_element_type=F32)
        dprobs = jnp.dot(v_wide, d_wide, preferred_element_type=F32)
        probs = jnp.exp2(scores * EXP_SCALE)
        dscores = (probs * dprobs).astype(BF16)
        v_sum = lax.dot_general(
            d_wide[:DIM], probs.astype(BF16), NT, preferred_element_type=F32
        )
        k_sum = lax.dot_general(q_wide[:DIM], dscores, NT, preferred_element_type=F32)
        k_turned = jnp.concatenate([kt[first_k + a] for a in range(4)], 1)
        q_sum = jnp.dot(k_turned, dscores, preferred_element_type=F32)
        for a in range(4):
            dv[first_k + a] += v_sum[:, a * ROWS : (a + 1) * ROWS]
            dk[first_k + a] += k_sum[:, a * ROWS : (a + 1) * ROWS]
            for head in range(2):
                col = (2 * a + head) * ROWS
                dq[first_q + a, pl.ds(head * DIM, DIM)] += q_sum[:, col : col + ROWS]

    q_tables = [table(q for q, _ in TILES[8 * half : 8 * half + 8]) for half in range(2)]
    k_tables = [table(k for _, k in TILES[8 * half : 8 * half + 8]) for half in range(2)]

    def run_half(half, carry):
        q_list = q_tables[0] + half * (q_tables[1] - q_tables[0])
        k_list = k_tables[0] + half * (k_tables[1] - k_tables[0])

        def run_tile(at, lists):
            q_list, k_list = lists
            step = half * 8 + at
            for n in range(16):
                pl.when(step == n)(functools.partial(before, n))
            tile(q_list % 4, k_list % 4)
            for n in range(16):
                pl.when(step == n)(functools.partial(after, n))
            return q_list // 4, k_list // 4

        lax.fori_loop(0, 8, run_tile, (q_list, k_list))
        return carry

    lax.fori_loop(0, 2, run_half, 0)

    for oz in range(1, NZ):
        dq_copies[oz].wait_recv()
    total = dq[0]
    for oz in range(1, NZ):
        total = total + dq_in[oz].astype(F32)
    total = total * SCALE
    for head in range(2):
        part = total[head * DIM : (head + 1) * DIM]
        query_grad[:, pl.ds(head * DIM, DIM)] = part.T.astype(BF16)
    for offset in plane_offsets:
        dkv_copies[offset].wait_recv()
    k_total, v_total = dk[0], dv[0]
    for slot in range(1, 16):
        k_total = k_total + dkv_in[slot, 0:DIM].astype(F32)
        v_total = v_total + dkv_in[slot, DIM:].astype(F32)
    key_grad[...] = (k_total * SCALE).T.astype(BF16)
    value_grad[...] = v_total.T.astype(BF16)

    for copies in (kv_copies, dkv_copies, dq_copies):
        for copy in copies.values():
            copy.wait_send()
    for copy in rights + lefts + pairs + sib_copies:
        copy.wait_send()


def body(query, key, value, out_grad, attn_out, lse, positions):
    vmem = pl.BlockSpec(memory_space=pltpu.VMEM)
    dma = pltpu.SemaphoreType.DMA
    return pl.pallas_call(
        kernel,
        out_shape=(
            jax.ShapeDtypeStruct((ROWS, 2 * DIM), BF16),
            jax.ShapeDtypeStruct((ROWS, DIM), BF16),
            jax.ShapeDtypeStruct((ROWS, DIM), BF16),
        ),
        in_specs=[vmem] * 7,
        out_specs=[vmem] * 3,
        scratch_shapes=[
            pltpu.VMEM((16, 4, DIM + AUG, ROWS), BF16),
            pltpu.VMEM((16, REST, ROWS), BF16),
            pltpu.VMEM((16, 2, ROWS, DIM), BF16),
            pltpu.VMEM((16, DIM, ROWS), BF16),
            pltpu.VMEM((16, ROWS, ROWS), BF16),
            pltpu.VMEM((32, ROWS), jnp.int32),
            pltpu.VMEM((16, 2 * DIM, ROWS), F32),
            pltpu.VMEM((16, DIM, ROWS), F32),
            pltpu.VMEM((16, DIM, ROWS), F32),
            pltpu.VMEM((8, 2 * DIM, ROWS), BF16),
            pltpu.VMEM((8, 2 * DIM, ROWS), BF16),
            pltpu.VMEM((8, 2 * DIM, ROWS), BF16),
            pltpu.VMEM((8, 2 * DIM, ROWS), BF16),
            pltpu.VMEM((16, 2 * DIM, ROWS), BF16),
            pltpu.VMEM((16, 2 * DIM, ROWS), BF16),
            dma((16,)),
            dma((16,)),
            dma((8,)),
            dma((17,)),
            dma((8,)),
            dma((8,)),
            dma((8,)),
            dma((8,)),
            dma((8,)),
            dma((16,)),
            dma((16,)),
        ],
        compiler_params=pltpu.CompilerParams(
            collective_id=0, has_side_effects=True, vmem_limit_bytes=56 * 2**20
        ),
    )(query, key, value, out_grad, attn_out, lse, positions.reshape(256, ROWS))


def solution(mesh):
    split = P(("row", "col"), None)
    return jax.shard_map(
        body,
        mesh=mesh,
        in_specs=(split,) * 6 + (P(),),
        out_specs=(split,) * 3,
        check_vma=False,
    )
```

```python
import functools
import math

import jax
import jax.numpy as jnp
from jax import lax
from jax.experimental import pallas as pl
from jax.experimental.pallas import tpu as pltpu
from jax.sharding import PartitionSpec as P

F32 = jnp.float32
BF16 = jnp.bfloat16
MESH = pl.DeviceIdType.MESH
ROWS = 128
DIM = 128
NX, NY, NZ = 4, 4, 8
AUG = 16
REST = 112
SCALE = 1.0 / math.sqrt(DIM)
EXP_SCALE = math.log2(math.e) / math.sqrt(DIM)
FAR = -1e30
NT = (((1,), (1,)), ((), ()))

PAIRS = ((0, 4), (1, 7), (2, 6), (3, 5))
SPOT = {oz: 2 * group + at for group, pair in enumerate(PAIRS) for at, oz in enumerate(pair)}

KEY_SPOTS = (
    (0, 0), (1, 0), (3, 0), (2, 0), (0, 1), (0, 3), (0, 2), (1, 1),
    (3, 1), (1, 3), (2, 1), (1, 2), (3, 3), (2, 3), (3, 2), (2, 2),
)

TILES = (
    (1, 0), (1, 1), (2, 0), (2, 1), (1, 2), (2, 2), (1, 3), (2, 3),
    (3, 2), (3, 3), (0, 2), (0, 3), (3, 1), (3, 0), (0, 1), (0, 0),
)


def table(values):
    total = 0
    for at, value in enumerate(values):
        total += value * 4**at
    return total


def place():
    row, col = lax.axis_index("row"), lax.axis_index("col")
    x, z_lo, core = col // 8, (col // 2) % 4, col % 2
    y, z_hi = row // 2, row % 2
    return x, y, z_hi * 4 + z_lo, core


def device(x, y, z, core):
    return (y * 2 + z // 4, x * 8 + (z % 4) * 2 + core)


def kernel(
    query, key, value, out_grad, attn_out, lse, positions,
    query_grad, key_grad, value_grad,
    pos, qd, qm, kv, kt, ka, kp, dq, dk, dv,
    sib_out, sib_in, dq_out, dq_in, dkv_out, dkv_in,
    pos_sem, kv_send, kv_recv, ring_send, q_recv, pair_send,
    sib_send, sib_recv, dq_send, dq_recv, dkv_send, dkv_recv,
):
    pos_copy = pltpu.make_async_copy(positions, pos, pos_sem)
    pos_copy.start()
    x, y, z, core = place()
    other = 1 - core

    def plane(ox, oy):
        return device((x + ox) % NX, (y + oy) % NY, z, core)

    def along(oz, which=None):
        return device(x, y, (z + oz) % NZ, core if which is None else which)

    sibling = device(x, y, z, other)

    barrier = pltpu.get_barrier_semaphore()
    peers = [plane(ox, oy) for ox, oy in KEY_SPOTS[1:]]
    peers += [along(oz) for oz in range(1, NZ)] + [sibling]
    for peer in peers:
        pl.semaphore_signal(barrier, inc=1, device_id=peer, device_id_type=MESH)

    kv[0, 0] = key[...]
    kv[0, 1] = value[...]
    line = lax.broadcasted_iota(jnp.int32, (AUG, ROWS), 0)

    def split_rows(term):
        high = term.astype(BF16).astype(F32)
        rest = term - high
        middle = rest.astype(BF16).astype(F32)
        low = rest - middle
        picked = jnp.where(line == 0, high, jnp.where(line == 1, middle, low))
        return jnp.where(line < 3, picked, 0.0).astype(BF16)

    for head in range(2):
        cut = pl.ds(head * DIM, DIM)
        grads, outs = out_grad[:, cut], attn_out[:, cut]
        delta = jnp.sum((grads.astype(F32) * outs.astype(F32)).T, axis=0, keepdims=True)
        qd[0, head, 0:DIM] = query[:, cut].T
        qd[0, head, DIM : DIM + AUG] = split_rows(lse[head : head + 1, :] * -math.sqrt(DIM))
        qd[0, 2 + head, 0:DIM] = grads.T
        qd[0, 2 + head, DIM : DIM + AUG] = split_rows(-delta)

    pl.semaphore_wait(barrier, len(peers))

    def own_slot(oz):
        return 2 * SPOT[oz % NZ]

    def ring_copy(hop, chunk, way):
        source, target = own_slot(way * (1 - hop)), own_slot(-way * hop)
        cut = pl.ds(2 * chunk, 2)
        return pltpu.make_async_remote_copy(
            src_ref=qd.at[source, cut],
            dst_ref=qd.at[target, cut],
            send_sem=ring_send.at[0 if way > 0 else 1, hop - 1, chunk],
            recv_sem=q_recv.at[target, chunk],
            device_id=along(way % NZ),
            device_id_type=MESH,
        )

    def pair_copy(oz, chunk):
        slot = own_slot(oz)
        cut = pl.ds(2 * chunk, 2)
        return pltpu.make_async_remote_copy(
            src_ref=qd.at[slot, cut],
            dst_ref=qd.at[slot + 1, cut],
            send_sem=pair_send.at[oz, chunk],
            recv_sem=q_recv.at[slot + 1, chunk],
            device_id=sibling,
            device_id_type=MESH,
        )

    ring = {
        (hop, chunk, way): ring_copy(hop, chunk, way)
        for hop in range(1, 5)
        for chunk in range(2)
        for way in (1, -1)
        if hop < 4 or (way > 0) == (chunk == 0)
    }
    pairs = {(oz, chunk): pair_copy(oz, chunk) for oz in range(NZ) for chunk in range(2)}

    def kv_copy(slot):
        ox, oy = KEY_SPOTS[slot]
        return pltpu.make_async_remote_copy(
            src_ref=kv.at[0],
            dst_ref=kv.at[slot],
            send_sem=kv_send.at[slot],
            recv_sem=kv_recv.at[slot],
            device_id=plane(NX - ox, NY - oy),
            device_id_type=MESH,
        )

    kv_copies = {slot: kv_copy(slot) for slot in range(1, 16)}

    def share_keys(group):
        for slot in range(4 * group, 4 * group + 4):
            if slot:
                kv_copies[slot].start()

    for chunk in range(2):
        for way in (1, -1):
            ring[(1, chunk, way)].start()
    share_keys(0)
    share_keys(1)
    for chunk in range(2):
        pairs[(0, chunk)].start()
    pos_copy.wait()

    dq[...] = jnp.zeros_like(dq)
    dk[...] = jnp.zeros_like(dk)
    dv[...] = jnp.zeros_like(dv)
    lane = lax.broadcasted_iota(jnp.int32, (ROWS, ROWS), 1)
    block = lax.broadcasted_iota(jnp.int32, (ROWS, ROWS), 0) // 64
    for slot in range(16):
        hot = (lane < 3) | (lane == AUG + 2 * slot + block)
        ka[slot] = jnp.where(hot, 1.0, 0.0).astype(BF16)
        r, c = plane(*KEY_SPOTS[slot])
        places = pos[pl.ds(r * 32 + c, 1), :] // 64
        kp[2 * slot : 2 * slot + 1, :] = jnp.broadcast_to(places[:, 0:1], (1, ROWS))
        kp[2 * slot + 1 : 2 * slot + 2, :] = jnp.broadcast_to(places[:, 64:65], (1, ROWS))
    for slot in range(16):
        r, c = along(PAIRS[slot // 4][slot // 2 % 2], other if slot % 2 else core)
        places = pos[pl.ds(r * 32 + c, 1), :] // 64
        bias = jnp.where(kp[...] < places, 0.0, FAR)
        qm[slot] = jnp.concatenate([bias, jnp.zeros((REST - 32, ROWS), F32)], 0).astype(BF16)

    none = jnp.zeros((REST, ROWS), BF16)

    def turn(slot):
        kt[slot] = kv[slot, 0].T

    turn(0)
    keys = jnp.concatenate([kv[0, 0], ka[0]], 1)
    values = jnp.concatenate([kv[0, 1], ka[0]], 1)
    q_own = [qd[0, head] for head in range(4)]
    q_cat = jnp.concatenate([jnp.concatenate([part, none], 0) for part in q_own[:2]], 1)
    d_cat = jnp.concatenate([jnp.concatenate([part, none], 0) for part in q_own[2:]], 1)
    scores = jnp.dot(keys, q_cat, preferred_element_type=F32)
    dprobs = jnp.dot(values, d_cat, preferred_element_type=F32)
    at_key = lax.broadcasted_iota(jnp.int32, (ROWS, 2 * ROWS), 0)
    at_row = lax.broadcasted_iota(jnp.int32, (ROWS, 2 * ROWS), 1) % ROWS
    inside = (at_key <= at_row) & (at_key // 64 == at_row // 64)
    probs = jnp.where(inside, jnp.exp2(scores * EXP_SCALE), 0.0)
    dscores = (probs * dprobs).astype(BF16)
    dv[0] = lax.dot_general(d_cat[:DIM], probs.astype(BF16), NT, preferred_element_type=F32)
    dk[0] = lax.dot_general(q_cat[:DIM], dscores, NT, preferred_element_type=F32)
    part = jnp.dot(kt[0], dscores, preferred_element_type=F32)
    dq[0] = jnp.concatenate([part[:, :ROWS], part[:, ROWS:]], 0)

    def wait_keys(group):
        for slot in range(4 * group, 4 * group + 4):
            if slot:
                kv_copies[slot].wait_recv()
                turn(slot)

    def dkv_copy(slot):
        return pltpu.make_async_remote_copy(
            src_ref=dkv_out.at[slot],
            dst_ref=dkv_in.at[slot],
            send_sem=dkv_send.at[slot],
            recv_sem=dkv_recv.at[slot],
            device_id=plane(*KEY_SPOTS[slot]),
            device_id_type=MESH,
        )

    dkv_copies = {slot: dkv_copy(slot) for slot in range(1, 16)}

    def send_keys(group):
        for slot in range(4 * group + 3, 4 * group - 1, -1):
            if slot:
                dkv_out[slot, 0:DIM] = dk[slot].astype(BF16)
                dkv_out[slot, DIM:] = dv[slot].astype(BF16)
                dkv_copies[slot].start()

    def sib_copy(oz):
        return pltpu.make_async_remote_copy(
            src_ref=sib_out.at[oz],
            dst_ref=sib_in.at[oz],
            send_sem=sib_send.at[oz],
            recv_sem=sib_recv.at[oz],
            device_id=sibling,
            device_id_type=MESH,
        )

    sib_copies = [sib_copy(oz) for oz in range(NZ)]

    def dq_copy(oz):
        return pltpu.make_async_remote_copy(
            src_ref=dq_out.at[oz],
            dst_ref=dq_in.at[NZ - oz],
            send_sem=dq_send.at[oz],
            recv_sem=dq_recv.at[NZ - oz],
            device_id=along(oz),
            device_id_type=MESH,
        )

    dq_copies = {oz: dq_copy(oz) for oz in range(1, NZ)}

    def swap_queries(group):
        for oz in PAIRS[group]:
            sib_out[oz] = dq[own_slot(oz) + 1].astype(BF16)
            sib_copies[oz].start()

    def send_queries(group):
        for oz in PAIRS[group]:
            sib_copies[oz].wait_recv()
            total = dq[own_slot(oz)] + sib_in[oz].astype(F32)
            if oz:
                dq_out[oz] = total.astype(BF16)
                dq_copies[oz].start()
            else:
                dq[0] = total

    def relay(hop, chunk):
        for way in (1, -1):
            if (hop, chunk, way) in ring:
                ring[(hop, chunk, way)].wait_recv()
                if (hop + 1, chunk, way) in ring:
                    ring[(hop + 1, chunk, way)].start()
                pairs[(-way * hop % NZ, chunk)].start()

    def wait_pairs(group):
        for oz in PAIRS[group]:
            for chunk in range(2):
                pairs[(oz, chunk)].wait_recv()

    def before(step):
        if step == 0:
            relay(1, 0)
            wait_keys(0)
            share_keys(2)
            share_keys(3)
            relay(1, 1)
            wait_pairs(1)
        if step == 1:
            relay(2, 0)
            wait_keys(1)
        if step == 2:
            relay(2, 1)
            wait_pairs(2)
        if step == 3:
            relay(3, 0)
        if step == 4:
            relay(3, 1)
            wait_keys(2)
        if step == 6:
            wait_keys(3)
        if step == 7:
            relay(4, 0)
            relay(4, 1)
        if step == 8:
            wait_pairs(3)
        if step == 10:
            wait_pairs(0)

    def after(step):
        if step == 6:
            swap_queries(1)
        if step == 7:
            send_queries(1)
            swap_queries(2)
        if step == 8:
            send_queries(2)
        if step == 10:
            send_keys(2)
        if step == 11:
            send_keys(3)
        if step == 13:
            swap_queries(3)
        if step == 14:
            send_queries(3)
            send_keys(1)
        if step == 15:
            swap_queries(0)
            send_keys(0)
            send_queries(0)

    def tile(at_q, at_k):
        first_q, first_k = at_q * 4, at_k * 4
        marks = ka[pl.ds(first_k, 4)].reshape(4 * ROWS, ROWS)
        k_part = kv[pl.ds(first_k, 4), 0].reshape(4 * ROWS, DIM)
        v_part = kv[pl.ds(first_k, 4), 1].reshape(4 * ROWS, DIM)
        k_wide = jnp.concatenate([k_part, marks], 1)
        v_wide = jnp.concatenate([v_part, marks], 1)
        q_cols = [
            jnp.concatenate([qd[first_q + a, head], qm[first_q + a]], 0)
            for a in range(4)
            for head in range(2)
        ]
        d_cols = [
            jnp.concatenate([qd[first_q + a, 2 + head], none], 0)
            for a in range(4)
            for head in range(2)
        ]
        q_wide = jnp.concatenate(q_cols, 1)
        d_wide = jnp.concatenate(d_cols, 1)
        scores = jnp.dot(k_wide, q_wide, preferred_element_type=F32)
        dprobs = jnp.dot(v_wide, d_wide, preferred_element_type=F32)
        probs = jnp.exp2(scores * EXP_SCALE)
        dscores = (probs * dprobs).astype(BF16)
        v_sum = lax.dot_general(
            d_wide[:DIM], probs.astype(BF16), NT, preferred_element_type=F32
        )
        k_sum = lax.dot_general(q_wide[:DIM], dscores, NT, preferred_element_type=F32)
        k_turned = jnp.concatenate([kt[first_k + a] for a in range(4)], 1)
        q_sum = jnp.dot(k_turned, dscores, preferred_element_type=F32)
        for a in range(4):
            dv[first_k + a] += v_sum[:, a * ROWS : (a + 1) * ROWS]
            dk[first_k + a] += k_sum[:, a * ROWS : (a + 1) * ROWS]
            for head in range(2):
                col = (2 * a + head) * ROWS
                dq[first_q + a, pl.ds(head * DIM, DIM)] += q_sum[:, col : col + ROWS]

    q_tables = [table(q for q, _ in TILES[8 * half : 8 * half + 8]) for half in range(2)]
    k_tables = [table(k for _, k in TILES[8 * half : 8 * half + 8]) for half in range(2)]

    def run_half(half, carry):
        q_list = q_tables[0] + half * (q_tables[1] - q_tables[0])
        k_list = k_tables[0] + half * (k_tables[1] - k_tables[0])

        def run_tile(at, lists):
            q_list, k_list = lists
            step = half * 8 + at
            for n in range(16):
                pl.when(step == n)(functools.partial(before, n))
            tile(q_list % 4, k_list % 4)
            for n in range(16):
                pl.when(step == n)(functools.partial(after, n))
            return q_list // 4, k_list // 4

        lax.fori_loop(0, 8, run_tile, (q_list, k_list))
        return carry

    lax.fori_loop(0, 2, run_half, 0)

    for oz in range(1, NZ):
        dq_copies[oz].wait_recv()
    total = dq[0]
    for oz in range(1, NZ):
        total = total + dq_in[oz].astype(F32)
    total = total * SCALE
    for head in range(2):
        part = total[head * DIM : (head + 1) * DIM]
        query_grad[:, pl.ds(head * DIM, DIM)] = part.T.astype(BF16)
    for slot in range(1, 16):
        dkv_copies[slot].wait_recv()
    k_total, v_total = dk[0], dv[0]
    for slot in range(1, 16):
        k_total = k_total + dkv_in[slot, 0:DIM].astype(F32)
        v_total = v_total + dkv_in[slot, DIM:].astype(F32)
    key_grad[...] = (k_total * SCALE).T.astype(BF16)
    value_grad[...] = v_total.T.astype(BF16)

    for copies in (kv_copies, dkv_copies, dq_copies, ring, pairs):
        for copy in copies.values():
            copy.wait_send()
    for copy in sib_copies:
        copy.wait_send()


def finish(q_in, k_in, v_in, q_out, k_out, v_out):
    q_out[...] = q_in[...]
    k_out[...] = k_in[...]
    v_out[...] = v_in[...]


def body(query, key, value, out_grad, attn_out, lse, positions):
    vmem = pl.BlockSpec(memory_space=pltpu.VMEM)
    dma = pltpu.SemaphoreType.DMA
    parts = pl.pallas_call(
        kernel,
        out_shape=(
            jax.ShapeDtypeStruct((ROWS, 2 * DIM), BF16),
            jax.ShapeDtypeStruct((ROWS, DIM), BF16),
            jax.ShapeDtypeStruct((ROWS, DIM), BF16),
        ),
        in_specs=[vmem] * 6 + [pl.BlockSpec(memory_space=pl.ANY)],
        out_specs=[vmem] * 3,
        scratch_shapes=[
            pltpu.VMEM((256, ROWS), jnp.int32),
            pltpu.VMEM((16, 4, DIM + AUG, ROWS), BF16),
            pltpu.VMEM((16, REST, ROWS), BF16),
            pltpu.VMEM((16, 2, ROWS, DIM), BF16),
            pltpu.VMEM((16, DIM, ROWS), BF16),
            pltpu.VMEM((16, ROWS, ROWS), BF16),
            pltpu.VMEM((32, ROWS), jnp.int32),
            pltpu.VMEM((16, 2 * DIM, ROWS), F32),
            pltpu.VMEM((16, DIM, ROWS), F32),
            pltpu.VMEM((16, DIM, ROWS), F32),
            pltpu.VMEM((8, 2 * DIM, ROWS), BF16),
            pltpu.VMEM((8, 2 * DIM, ROWS), BF16),
            pltpu.VMEM((8, 2 * DIM, ROWS), BF16),
            pltpu.VMEM((8, 2 * DIM, ROWS), BF16),
            pltpu.VMEM((16, 2 * DIM, ROWS), BF16),
            pltpu.VMEM((16, 2 * DIM, ROWS), BF16),
            dma,
            dma((16,)),
            dma((16,)),
            dma((2, 4, 2)),
            dma((16, 2)),
            dma((8, 2)),
            dma((8,)),
            dma((8,)),
            dma((8,)),
            dma((8,)),
            dma((16,)),
            dma((16,)),
        ],
        compiler_params=pltpu.CompilerParams(
            collective_id=0, has_side_effects=True, vmem_limit_bytes=56 * 2**20
        ),
    )(query, key, value, out_grad, attn_out, lse.T, positions.reshape(256, ROWS))
    return pl.pallas_call(
        finish,
        out_shape=tuple(jax.ShapeDtypeStruct(part.shape, part.dtype) for part in parts),
        in_specs=[vmem] * 3,
        out_specs=[vmem] * 3,
    )(*parts)


def solution(mesh):
    split = P(("row", "col"), None)
    return jax.shard_map(
        body,
        mesh=mesh,
        in_specs=(split,) * 6 + (P(),),
        out_specs=(split,) * 3,
        check_vma=False,
    )
```

```python
import functools
import math

import jax
import jax.numpy as jnp
from jax import lax
from jax.experimental import pallas as pl
from jax.experimental.pallas import tpu as pltpu
from jax.sharding import PartitionSpec as P

F32 = jnp.float32
BF16 = jnp.bfloat16
MESH = pl.DeviceIdType.MESH
ROWS = 128
DIM = 128
NX, NY, NZ = 4, 4, 8
AUG = 16
REST = 112
SCALE = 1.0 / math.sqrt(DIM)
EXP_SCALE = math.log2(math.e) / math.sqrt(DIM)
FAR = -1e30
NT = (((1,), (1,)), ((), ()))

PAIRS = ((0, 4), (1, 7), (2, 6), (3, 5))
SPOT = {oz: 2 * group + at for group, pair in enumerate(PAIRS) for at, oz in enumerate(pair)}

KEY_SPOTS = (
    (0, 0), (1, 0), (3, 0), (2, 0), (0, 1), (0, 3), (0, 2), (1, 1),
    (3, 1), (1, 3), (2, 1), (1, 2), (3, 3), (2, 3), (3, 2), (2, 2),
)

TILES = (
    (0, 1, 0), (0, 1, 1), (0, 2, 0), (0, 2, 1), (0, 1, 2), (0, 2, 2), (0, 1, 3), (0, 2, 3),
    (0, 3, 2), (0, 3, 3), (0, 0, 2), (0, 0, 3), (0, 3, 1), (0, 3, 0), (0, 0, 1), (0, 0, 0),
)


def table(values):
    total = 0
    for at, value in enumerate(values):
        total += value * 4**at
    return total


def kernel(
    query, key, value, out_grad, attn_out, lse, positions,
    query_grad, key_grad, value_grad,
    pos, qd, qm, kv, kt, ka, kp, dq, dk, dv,
    sib_out, sib_in, dq_out, dq_in, dkv_out, dkv_in,
    pos_sem, kv_send, kv_recv, ring_send, q_recv, pair_send,
    sib_send, sib_recv, dq_send, dq_recv, dkv_send, dkv_recv,
):
    pos_copy = pltpu.make_async_copy(positions, pos, pos_sem)
    pos_copy.start()
    row, col = lax.axis_index("row"), lax.axis_index("col")
    core = lax.rem(col, 2)
    other = 1 - core
    x, z_lo = lax.div(col, 8), lax.rem(lax.div(col, 2), 4)
    y, z_hi = lax.div(row, 2), lax.rem(row, 2)
    z = z_hi * 4 + z_lo
    rows_y = [lax.rem(y + oy, NY) * 2 for oy in range(NY)]
    cols_x = [lax.rem(x + ox, NX) * 8 for ox in range(NX)]
    zs = [lax.rem(z + oz, NZ) for oz in range(NZ)]
    rows_z = [lax.div(one, 4) for one in zs]
    cols_z = [lax.rem(one, 4) * 2 for one in zs]

    def plane(ox, oy):
        return (rows_y[oy % NY] + z_hi, cols_x[ox % NX] + (z_lo * 2 + core))

    def along(oz, which=None):
        return (rows_y[0] + rows_z[oz % NZ], cols_x[0] + cols_z[oz % NZ] + (core if which is None else which))

    sibling = (row, col + 1 - 2 * core)

    barrier = pltpu.get_barrier_semaphore()
    peers = [plane(ox, oy) for ox, oy in KEY_SPOTS[1:]]
    peers += [along(oz) for oz in range(1, NZ)] + [sibling]
    for peer in peers:
        pl.semaphore_signal(barrier, inc=1, device_id=peer, device_id_type=MESH)

    kv[0, 0] = key[...]
    kv[0, 1] = value[...]
    line = lax.broadcasted_iota(jnp.int32, (AUG, ROWS), 0)

    def split_rows(term):
        high = term.astype(BF16).astype(F32)
        rest = term - high
        middle = rest.astype(BF16).astype(F32)
        low = rest - middle
        picked = jnp.where(line == 0, high, jnp.where(line == 1, middle, low))
        return jnp.where(line < 3, picked, 0.0).astype(BF16)

    for head in range(2):
        cut = pl.ds(head * DIM, DIM)
        grads, outs = out_grad[:, cut], attn_out[:, cut]
        delta = jnp.sum((grads.astype(F32) * outs.astype(F32)).T, axis=0, keepdims=True)
        qd[0, head, 0:DIM] = query[:, cut].T
        qd[0, head, DIM : DIM + AUG] = split_rows(lse[head : head + 1, :] * -math.sqrt(DIM))
        qd[0, 2 + head, 0:DIM] = grads.T
        qd[0, 2 + head, DIM : DIM + AUG] = split_rows(-delta)

    pl.semaphore_wait(barrier, len(peers))

    def own_slot(oz):
        return 2 * SPOT[oz % NZ]

    def ring_copy(hop, chunk, way):
        far = max(hop - 2, 1)
        source, target = own_slot(way * (far - hop)), own_slot(-way * hop)
        cut = pl.ds(2 * chunk, 2)
        return pltpu.make_async_remote_copy(
            src_ref=qd.at[source, cut],
            dst_ref=qd.at[target, cut],
            send_sem=ring_send.at[0 if way > 0 else 1, hop - 1, chunk],
            recv_sem=q_recv.at[target, chunk],
            device_id=along(way * far),
            device_id_type=MESH,
        )

    def pair_copy(oz, chunk):
        slot = own_slot(oz)
        cut = pl.ds(2 * chunk, 2)
        return pltpu.make_async_remote_copy(
            src_ref=qd.at[slot, cut],
            dst_ref=qd.at[slot + 1, cut],
            send_sem=pair_send.at[oz, chunk],
            recv_sem=q_recv.at[slot + 1, chunk],
            device_id=sibling,
            device_id_type=MESH,
        )

    ring = {
        (hop, chunk, way): ring_copy(hop, chunk, way)
        for hop in range(1, 5)
        for chunk in range(2)
        for way in (1, -1)
        if hop < 4 or (way > 0) == (chunk == 0)
    }
    pairs = {(oz, chunk): pair_copy(oz, chunk) for oz in range(NZ) for chunk in range(2)}

    def kv_copy(slot):
        ox, oy = KEY_SPOTS[slot]
        return pltpu.make_async_remote_copy(
            src_ref=kv.at[0],
            dst_ref=kv.at[slot],
            send_sem=kv_send.at[slot, 0],
            recv_sem=kv_recv.at[slot, 0],
            device_id=plane(-ox, -oy),
            device_id_type=MESH,
        )

    def kv_relay(slot, part):
        ox, oy = KEY_SPOTS[slot]
        middle = KEY_SPOTS.index((0, oy) if part else (ox, 0))
        return pltpu.make_async_remote_copy(
            src_ref=kv.at[middle, part],
            dst_ref=kv.at[slot, part],
            send_sem=kv_send.at[slot, part],
            recv_sem=kv_recv.at[slot, part],
            device_id=plane(-ox, 0) if part else plane(0, -oy),
            device_id_type=MESH,
        )

    kv_copies = {slot: kv_copy(slot) for slot in range(1, 8)}
    kv_relays = {(slot, part): kv_relay(slot, part) for slot in range(8, 16) for part in range(2)}

    def share_keys(group):
        for slot in range(4 * group, 4 * group + 4):
            if slot:
                kv_copies[slot].start()

    def relay_keys(part):
        for slot in range(8, 16):
            kv_relays[(slot, part)].start()

    for chunk in range(2):
        for way in (1, -1):
            ring[(1, chunk, way)].start()
    share_keys(0)
    share_keys(1)
    for chunk in range(2):
        pairs[(0, chunk)].start()
    pos_copy.wait()

    dq[...] = jnp.zeros_like(dq)
    dk[...] = jnp.zeros_like(dk)
    dv[...] = jnp.zeros_like(dv)
    lane = lax.broadcasted_iota(jnp.int32, (ROWS, ROWS), 1)
    block = lax.broadcasted_iota(jnp.int32, (ROWS, ROWS), 0) // 64
    for slot in range(16):
        hot = (lane < 3) | (lane == AUG + 2 * slot + block)
        ka[slot] = jnp.where(hot, 1.0, 0.0).astype(BF16)
        r, c = plane(*KEY_SPOTS[slot])
        places = pos[pl.ds(r * 32 + c, 1), :] // 64
        kp[2 * slot : 2 * slot + 1, :] = jnp.broadcast_to(places[:, 0:1], (1, ROWS))
        kp[2 * slot + 1 : 2 * slot + 2, :] = jnp.broadcast_to(places[:, 64:65], (1, ROWS))
    for slot in range(16):
        r, c = along(PAIRS[slot // 4][slot // 2 % 2], other if slot % 2 else core)
        places = pos[pl.ds(r * 32 + c, 1), :] // 64
        bias = jnp.where(kp[...] < places, 0.0, FAR)
        qm[slot] = jnp.concatenate([bias, jnp.zeros((REST - 32, ROWS), F32)], 0).astype(BF16)

    none = jnp.zeros((REST, ROWS), BF16)

    def turn(slot):
        kt[slot] = kv[slot, 0].T

    turn(0)
    keys = jnp.concatenate([kv[0, 0], ka[0]], 1)
    values = jnp.concatenate([kv[0, 1], ka[0]], 1)
    q_own = [qd[0, head] for head in range(4)]
    q_cat = jnp.concatenate([jnp.concatenate([part, none], 0) for part in q_own[:2]], 1)
    d_cat = jnp.concatenate([jnp.concatenate([part, none], 0) for part in q_own[2:]], 1)
    scores = jnp.dot(keys, q_cat, preferred_element_type=F32)
    dprobs = jnp.dot(values, d_cat, preferred_element_type=F32)
    at_key = lax.broadcasted_iota(jnp.int32, (ROWS, 2 * ROWS), 0)
    at_row = lax.broadcasted_iota(jnp.int32, (ROWS, 2 * ROWS), 1) % ROWS
    inside = (at_key <= at_row) & (at_key // 64 == at_row // 64)
    probs = jnp.where(inside, jnp.exp2(scores * EXP_SCALE), 0.0)
    dscores = (probs * dprobs).astype(BF16)
    dv[0] = lax.dot_general(probs.astype(BF16), d_cat[:DIM], NT, preferred_element_type=F32)
    dk[0] = lax.dot_general(dscores, q_cat[:DIM], NT, preferred_element_type=F32)
    part = jnp.dot(kt[0], dscores, preferred_element_type=F32)
    dq[0] = jnp.concatenate([part[:, :ROWS], part[:, ROWS:]], 0)

    def wait_keys(group):
        for slot in range(4 * group, 4 * group + 4):
            if slot in kv_copies:
                kv_copies[slot].wait_recv()
            if (slot, 0) in kv_relays:
                kv_relays[(slot, 0)].wait_recv()
                kv_relays[(slot, 1)].wait_recv()
            if slot:
                turn(slot)

    def dkv_copy(slot):
        return pltpu.make_async_remote_copy(
            src_ref=dkv_out.at[slot],
            dst_ref=dkv_in.at[slot],
            send_sem=dkv_send.at[slot],
            recv_sem=dkv_recv.at[slot],
            device_id=plane(*KEY_SPOTS[slot]),
            device_id_type=MESH,
        )

    dkv_copies = {slot: dkv_copy(slot) for slot in range(1, 16)}

    def send_keys(group):
        for slot in range(4 * group + 3, 4 * group - 1, -1):
            if slot:
                dkv_out[slot, 0:DIM] = dk[slot].astype(BF16)
                dkv_out[slot, DIM:] = dv[slot].astype(BF16)
                dkv_copies[slot].start()

    def sib_copy(oz):
        return pltpu.make_async_remote_copy(
            src_ref=sib_out.at[oz],
            dst_ref=sib_in.at[oz],
            send_sem=sib_send.at[oz],
            recv_sem=sib_recv.at[oz],
            device_id=sibling,
            device_id_type=MESH,
        )

    sib_copies = [sib_copy(oz) for oz in range(NZ)]

    def dq_copy(oz):
        return pltpu.make_async_remote_copy(
            src_ref=dq_out.at[oz],
            dst_ref=dq_in.at[NZ - oz],
            send_sem=dq_send.at[oz],
            recv_sem=dq_recv.at[NZ - oz],
            device_id=along(oz),
            device_id_type=MESH,
        )

    dq_copies = {oz: dq_copy(oz) for oz in range(1, NZ)}

    def swap_queries(*offsets):
        for oz in offsets:
            sib_out[oz] = dq[own_slot(oz) + 1].astype(BF16)
            sib_copies[oz].start()

    def send_queries(*offsets):
        for oz in offsets:
            sib_copies[oz].wait_recv()
            total = dq[own_slot(oz)] + sib_in[oz].astype(F32)
            if oz:
                dq_out[oz] = total.astype(BF16)
                dq_copies[oz].start()
            else:
                dq[0] = total

    def relay(hop, chunk):
        for way in (1, -1):
            if (hop, chunk, way) in ring:
                ring[(hop, chunk, way)].wait_recv()
                for later in {1: (2,), 2: (3, 4)}.get(hop, ()):
                    if (later, chunk, way) in ring:
                        ring[(later, chunk, way)].start()
                pairs[(-way * hop % NZ, chunk)].start()

    def wait_pairs(*offsets):
        for oz in offsets:
            for chunk in range(2):
                pairs[(oz, chunk)].wait_recv()

    def before(step):
        if step == 0:
            relay(1, 0)
            relay(1, 1)
            wait_keys(0)
            relay_keys(0)
            wait_pairs(1, 7)
        if step == 1:
            wait_keys(1)
            relay_keys(1)
            relay(2, 0)
        if step == 2:
            relay(2, 1)
            wait_pairs(2, 6)
        if step == 4:
            wait_keys(2)
        if step == 5:
            relay(3, 0)
        if step == 6:
            relay(3, 1)
            wait_keys(3)
        if step == 7:
            relay(4, 0)
            relay(4, 1)
        if step == 8:
            wait_pairs(3, 5)
        if step == 10:
            wait_pairs(0, 4)

    def after(step):
        if step == 6:
            swap_queries(1, 7)
        if step == 7:
            send_queries(1, 7)
            swap_queries(2, 6)
        if step == 8:
            send_queries(2, 6)
        if step == 10:
            send_keys(2)
        if step == 11:
            send_keys(3)
        if step == 13:
            swap_queries(3, 5)
        if step == 14:
            send_queries(3, 5)
            send_keys(1)
        if step == 15:
            swap_queries(4, 0)
            send_keys(0)
            send_queries(4, 0)

    def between(step):
        if step:
            after(step - 1)
        before(step)

    def tile(first_q, n_q, first_k, n_k):
        marks = ka[pl.ds(first_k, n_k)].reshape(n_k * ROWS, ROWS)
        k_part = kv[pl.ds(first_k, n_k), 0].reshape(n_k * ROWS, DIM)
        v_part = kv[pl.ds(first_k, n_k), 1].reshape(n_k * ROWS, DIM)
        k_wide = jnp.concatenate([k_part, marks], 1)
        v_wide = jnp.concatenate([v_part, marks], 1)
        q_cols = [
            jnp.concatenate([qd[first_q + a, head], qm[first_q + a]], 0)
            for a in range(n_q)
            for head in range(2)
        ]
        d_cols = [
            jnp.concatenate([qd[first_q + a, 2 + head], none], 0)
            for a in range(n_q)
            for head in range(2)
        ]
        q_wide = jnp.concatenate(q_cols, 1)
        d_wide = jnp.concatenate(d_cols, 1)
        scores = jnp.dot(k_wide, q_wide, preferred_element_type=F32)
        dprobs = jnp.dot(v_wide, d_wide, preferred_element_type=F32)
        probs = jnp.exp2(scores * EXP_SCALE)
        dscores = (probs * dprobs).astype(BF16)
        v_sum = lax.dot_general(
            probs.astype(BF16), d_wide[:DIM], NT, preferred_element_type=F32
        )
        k_sum = lax.dot_general(dscores, q_wide[:DIM], NT, preferred_element_type=F32)
        k_turned = jnp.concatenate([kt[first_k + a] for a in range(n_k)], 1)
        q_sum = jnp.dot(k_turned, dscores, preferred_element_type=F32)
        for a in range(n_k):
            dv[first_k + a] += v_sum[a * ROWS : (a + 1) * ROWS]
            dk[first_k + a] += k_sum[a * ROWS : (a + 1) * ROWS]
        for a in range(n_q):
            for head in range(2):
                col = (2 * a + head) * ROWS
                dq[first_q + a, pl.ds(head * DIM, DIM)] += q_sum[:, col : col + ROWS]

    tables = [
        [table(entry[part] for entry in TILES[8 * half : 8 * half + 8]) for part in range(3)]
        for half in range(2)
    ]

    def run_half(half, carry):
        lists = tuple(one + half * (two - one) for one, two in zip(*tables))

        def run_tile(at, lists):
            _, q_part, k_part = (one % 4 for one in lists)
            step = half * 8 + at
            for part in range(4):

                @pl.when(at // 2 == part)
                def _():
                    for n in (2 * part, 2 * part + 1, 2 * part + 8, 2 * part + 9):
                        pl.when(step == n)(functools.partial(between, n))

            tile(q_part * 4, 4, k_part * 4, 4)
            return tuple(one // 4 for one in lists)

        lax.fori_loop(0, 8, run_tile, lists)
        return carry

    lax.fori_loop(0, 2, run_half, 0)
    after(15)

    for oz in range(1, NZ):
        dq_copies[oz].wait_recv()
    total = dq[0]
    for oz in range(1, NZ):
        total = total + dq_in[oz].astype(F32)
    total = total * SCALE
    for head in range(2):
        part = total[head * DIM : (head + 1) * DIM]
        query_grad[:, pl.ds(head * DIM, DIM)] = part.T.astype(BF16)
    for slot in range(1, 16):
        dkv_copies[slot].wait_recv()
    k_total, v_total = dk[0], dv[0]
    for slot in range(1, 16):
        k_total = k_total + dkv_in[slot, 0:DIM].astype(F32)
        v_total = v_total + dkv_in[slot, DIM:].astype(F32)
    key_grad[...] = (k_total * SCALE).astype(BF16)
    value_grad[...] = v_total.astype(BF16)

    for copies in (kv_copies, kv_relays, dkv_copies, dq_copies, ring, pairs):
        for copy in copies.values():
            copy.wait_send()
    for copy in sib_copies:
        copy.wait_send()


def finish(q_in, k_in, v_in, q_out, k_out, v_out):
    q_out[...] = q_in[...]
    k_out[...] = k_in[...]
    v_out[...] = v_in[...]


def body(query, key, value, out_grad, attn_out, lse, positions):
    vmem = pl.BlockSpec(memory_space=pltpu.VMEM)
    dma = pltpu.SemaphoreType.DMA
    parts = pl.pallas_call(
        kernel,
        out_shape=(
            jax.ShapeDtypeStruct((ROWS, 2 * DIM), BF16),
            jax.ShapeDtypeStruct((ROWS, DIM), BF16),
            jax.ShapeDtypeStruct((ROWS, DIM), BF16),
        ),
        in_specs=[vmem] * 6 + [pl.BlockSpec(memory_space=pl.ANY)],
        out_specs=[vmem] * 3,
        scratch_shapes=[
            pltpu.VMEM((256, ROWS), jnp.int32),
            pltpu.VMEM((16, 4, DIM + AUG, ROWS), BF16),
            pltpu.VMEM((16, REST, ROWS), BF16),
            pltpu.VMEM((16, 2, ROWS, DIM), BF16),
            pltpu.VMEM((16, DIM, ROWS), BF16),
            pltpu.VMEM((16, ROWS, ROWS), BF16),
            pltpu.VMEM((32, ROWS), jnp.int32),
            pltpu.VMEM((16, 2 * DIM, ROWS), F32),
            pltpu.VMEM((16, DIM, ROWS), F32),
            pltpu.VMEM((16, DIM, ROWS), F32),
            pltpu.VMEM((8, 2 * DIM, ROWS), BF16),
            pltpu.VMEM((8, 2 * DIM, ROWS), BF16),
            pltpu.VMEM((8, 2 * DIM, ROWS), BF16),
            pltpu.VMEM((8, 2 * DIM, ROWS), BF16),
            pltpu.VMEM((16, 2 * DIM, ROWS), BF16),
            pltpu.VMEM((16, 2 * DIM, ROWS), BF16),
            dma,
            dma((16, 2)),
            dma((16, 2)),
            dma((2, 4, 2)),
            dma((16, 2)),
            dma((8, 2)),
            dma((8,)),
            dma((8,)),
            dma((8,)),
            dma((8,)),
            dma((16,)),
            dma((16,)),
        ],
        compiler_params=pltpu.CompilerParams(
            collective_id=0, has_side_effects=True, vmem_limit_bytes=56 * 2**20
        ),
    )(query, key, value, out_grad, attn_out, lse.T, positions.reshape(256, ROWS))
    return pl.pallas_call(
        finish,
        out_shape=tuple(jax.ShapeDtypeStruct(part.shape, part.dtype) for part in parts),
        in_specs=[vmem] * 3,
        out_specs=[vmem] * 3,
    )(*parts)


def solution(mesh):
    split = P(("row", "col"), None)
    return jax.shard_map(
        body,
        mesh=mesh,
        in_specs=(split,) * 6 + (P(),),
        out_specs=(split,) * 3,
        check_vma=False,
    )
```

```python
import functools
import math

import jax
import jax.numpy as jnp
from jax import lax
from jax.experimental import pallas as pl
from jax.experimental.pallas import tpu as pltpu
from jax.sharding import PartitionSpec as P

F32 = jnp.float32
BF16 = jnp.bfloat16
MESH = pl.DeviceIdType.MESH
ROWS = 128
DIM = 128
NX, NY, NZ = 4, 4, 8
AUG = 16
REST = 112
SCALE = 1.0 / math.sqrt(DIM)
EXP_SCALE = math.log2(math.e) / math.sqrt(DIM)
FAR = -1e30
NT = (((1,), (1,)), ((), ()))

PAIRS = ((0, 4), (1, 7), (2, 6), (3, 5))
SPOT = {oz: 2 * group + at for group, pair in enumerate(PAIRS) for at, oz in enumerate(pair)}

KEY_SPOTS = (
    (0, 0), (1, 0), (3, 0), (2, 0), (0, 1), (0, 3), (0, 2), (1, 1),
    (3, 1), (1, 3), (2, 1), (1, 2), (3, 3), (2, 3), (3, 2), (2, 2),
)

TILES = (
    (0, 1, 0), (0, 1, 1), (0, 2, 0), (0, 2, 1), (0, 1, 2), (0, 2, 2), (0, 1, 3), (0, 2, 3),
    (0, 3, 2), (0, 3, 3), (0, 0, 2), (0, 0, 3), (0, 3, 1), (0, 3, 0), (0, 0, 1), (0, 0, 0),
)


def table(values):
    total = 0
    for at, value in enumerate(values):
        total += value * 4**at
    return total


def kernel(
    query, key, value, out_grad, attn_out, lse, positions,
    query_grad, key_grad, value_grad,
    pos, qd, qm, kv, kt, ka, kp, dq, dk, dv,
    sib_out, sib_in, dq_out, dq_in, dkv_out, dkv_in,
    pos_sem, kv_send, kv_recv, ring_send, q_recv, pair_send,
    sib_send, sib_recv, dq_send, dq_recv, dkv_send, dkv_recv, met,
):
    pos_copy = pltpu.make_async_copy(positions, pos, pos_sem)
    pos_copy.start()
    row, col = lax.axis_index("row"), lax.axis_index("col")
    core = lax.rem(col, 2)
    other = 1 - core
    x, z_lo = lax.div(col, 8), lax.rem(lax.div(col, 2), 4)
    y, z_hi = lax.div(row, 2), lax.rem(row, 2)
    z = z_hi * 4 + z_lo
    rows_y = [lax.rem(y + oy, NY) * 2 for oy in range(NY)]
    cols_x = [lax.rem(x + ox, NX) * 8 for ox in range(NX)]
    zs = [lax.rem(z + oz, NZ) for oz in range(NZ)]
    rows_z = [lax.div(one, 4) for one in zs]
    cols_z = [lax.rem(one, 4) * 2 for one in zs]

    def plane(ox, oy):
        return (rows_y[oy % NY] + z_hi, cols_x[ox % NX] + (z_lo * 2 + core))

    def along(oz, which=None):
        return (rows_y[0] + rows_z[oz % NZ], cols_x[0] + cols_z[oz % NZ] + (core if which is None else which))

    sibling = (row, col + 1 - 2 * core)

    barrier = pltpu.get_barrier_semaphore()
    near = [along(1), along(-1), plane(1, 0), plane(-1, 0), plane(0, 1), plane(0, -1), sibling]
    for peer in near:
        pl.semaphore_signal(barrier, inc=1, device_id=peer, device_id_type=MESH)

    def greet(turn):
        for peer in near:
            pl.semaphore_signal(met.at[turn], inc=1, device_id=peer, device_id_type=MESH)


    kv[0, 0] = key[...]
    kv[0, 1] = value[...]
    line = lax.broadcasted_iota(jnp.int32, (AUG, ROWS), 0)

    def split_rows(term):
        high = term.astype(BF16).astype(F32)
        rest = term - high
        middle = rest.astype(BF16).astype(F32)
        low = rest - middle
        picked = jnp.where(line == 0, high, jnp.where(line == 1, middle, low))
        return jnp.where(line < 3, picked, 0.0).astype(BF16)

    for head in range(2):
        cut = pl.ds(head * DIM, DIM)
        grads, outs = out_grad[:, cut], attn_out[:, cut]
        delta = jnp.sum((grads.astype(F32) * outs.astype(F32)).T, axis=0, keepdims=True)
        qd[0, head, 0:DIM] = query[:, cut].T
        qd[0, head, DIM : DIM + AUG] = split_rows(lse[head : head + 1, :] * -math.sqrt(DIM))
        qd[0, 2 + head, 0:DIM] = grads.T
        qd[0, 2 + head, DIM : DIM + AUG] = split_rows(-delta)

    pl.semaphore_wait(barrier, len(near))

    def own_slot(oz):
        return 2 * SPOT[oz % NZ]

    def ring_copy(hop, chunk, way):
        far = max(hop - 2, 1)
        source, target = own_slot(way * (far - hop)), own_slot(-way * hop)
        cut = pl.ds(2 * chunk, 2)
        return pltpu.make_async_remote_copy(
            src_ref=qd.at[source, cut],
            dst_ref=qd.at[target, cut],
            send_sem=ring_send.at[0 if way > 0 else 1, hop - 1, chunk],
            recv_sem=q_recv.at[target, chunk],
            device_id=along(way * far),
            device_id_type=MESH,
        )

    def pair_copy(oz, chunk):
        slot = own_slot(oz)
        cut = pl.ds(2 * chunk, 2)
        return pltpu.make_async_remote_copy(
            src_ref=qd.at[slot, cut],
            dst_ref=qd.at[slot + 1, cut],
            send_sem=pair_send.at[oz, chunk],
            recv_sem=q_recv.at[slot + 1, chunk],
            device_id=sibling,
            device_id_type=MESH,
        )

    ring = {
        (hop, chunk, way): ring_copy(hop, chunk, way)
        for hop in range(1, 5)
        for chunk in range(2)
        for way in (1, -1)
        if hop < 4 or (way > 0) == (chunk == 0)
    }
    pairs = {(oz, chunk): pair_copy(oz, chunk) for oz in range(NZ) for chunk in range(2)}

    def kv_copy(slot):
        ox, oy = KEY_SPOTS[slot]
        return pltpu.make_async_remote_copy(
            src_ref=kv.at[0],
            dst_ref=kv.at[slot],
            send_sem=kv_send.at[slot, 0],
            recv_sem=kv_recv.at[slot, 0],
            device_id=plane(-ox, -oy),
            device_id_type=MESH,
        )

    def kv_relay(slot, part):
        ox, oy = KEY_SPOTS[slot]
        middle = KEY_SPOTS.index((0, oy) if part else (ox, 0))
        return pltpu.make_async_remote_copy(
            src_ref=kv.at[middle, part],
            dst_ref=kv.at[slot, part],
            send_sem=kv_send.at[slot, part],
            recv_sem=kv_recv.at[slot, part],
            device_id=plane(-ox, 0) if part else plane(0, -oy),
            device_id_type=MESH,
        )

    kv_copies = {slot: kv_copy(slot) for slot in range(1, 8)}
    kv_relays = {(slot, part): kv_relay(slot, part) for slot in range(8, 16) for part in range(2)}

    def relay_keys(part):
        for slot in range(8, 16):
            kv_relays[(slot, part)].start()

    for chunk in range(2):
        for way in (1, -1):
            ring[(1, chunk, way)].start()
    for slot in (1, 2, 4, 5):
        kv_copies[slot].start()
    for chunk in range(2):
        pairs[(0, chunk)].start()
    greet(0)
    pos_copy.wait()

    dq[...] = jnp.zeros_like(dq)
    dk[...] = jnp.zeros_like(dk)
    dv[...] = jnp.zeros_like(dv)
    lane = lax.broadcasted_iota(jnp.int32, (ROWS, ROWS), 1)
    block = lax.broadcasted_iota(jnp.int32, (ROWS, ROWS), 0) // 64
    for slot in range(16):
        hot = (lane < 3) | (lane == AUG + 2 * slot + block)
        ka[slot] = jnp.where(hot, 1.0, 0.0).astype(BF16)
        r, c = plane(*KEY_SPOTS[slot])
        places = pos[pl.ds(r * 32 + c, 1), :] // 64
        kp[2 * slot : 2 * slot + 1, :] = jnp.broadcast_to(places[:, 0:1], (1, ROWS))
        kp[2 * slot + 1 : 2 * slot + 2, :] = jnp.broadcast_to(places[:, 64:65], (1, ROWS))
    for slot in range(16):
        r, c = along(PAIRS[slot // 4][slot // 2 % 2], other if slot % 2 else core)
        places = pos[pl.ds(r * 32 + c, 1), :] // 64
        bias = jnp.where(kp[...] < places, 0.0, FAR)
        qm[slot] = jnp.concatenate([bias, jnp.zeros((REST - 32, ROWS), F32)], 0).astype(BF16)

    pl.semaphore_wait(met.at[0], len(near))
    for slot in (3, 6, 7):
        kv_copies[slot].start()
    greet(1)

    none = jnp.zeros((REST, ROWS), BF16)

    def turn(slot):
        kt[slot] = kv[slot, 0].T

    turn(0)
    keys = jnp.concatenate([kv[0, 0], ka[0]], 1)
    values = jnp.concatenate([kv[0, 1], ka[0]], 1)
    q_own = [qd[0, head] for head in range(4)]
    q_cat = jnp.concatenate([jnp.concatenate([part, none], 0) for part in q_own[:2]], 1)
    d_cat = jnp.concatenate([jnp.concatenate([part, none], 0) for part in q_own[2:]], 1)
    scores = jnp.dot(keys, q_cat, preferred_element_type=F32)
    dprobs = jnp.dot(values, d_cat, preferred_element_type=F32)
    at_key = lax.broadcasted_iota(jnp.int32, (ROWS, 2 * ROWS), 0)
    at_row = lax.broadcasted_iota(jnp.int32, (ROWS, 2 * ROWS), 1) % ROWS
    inside = (at_key <= at_row) & (at_key // 64 == at_row // 64)
    probs = jnp.where(inside, jnp.exp2(scores * EXP_SCALE), 0.0)
    dscores = (probs * dprobs).astype(BF16)
    dv[0] = lax.dot_general(probs.astype(BF16), d_cat[:DIM], NT, preferred_element_type=F32)
    dk[0] = lax.dot_general(dscores, q_cat[:DIM], NT, preferred_element_type=F32)
    part = jnp.dot(kt[0], dscores, preferred_element_type=F32)
    dq[0] = jnp.concatenate([part[:, :ROWS], part[:, ROWS:]], 0)

    def wait_keys(group):
        for slot in range(4 * group, 4 * group + 4):
            if slot in kv_copies:
                kv_copies[slot].wait_recv()
            if (slot, 0) in kv_relays:
                kv_relays[(slot, 0)].wait_recv()
                kv_relays[(slot, 1)].wait_recv()
            if slot:
                turn(slot)

    def dkv_copy(slot):
        return pltpu.make_async_remote_copy(
            src_ref=dkv_out.at[slot],
            dst_ref=dkv_in.at[slot],
            send_sem=dkv_send.at[slot],
            recv_sem=dkv_recv.at[slot],
            device_id=plane(*KEY_SPOTS[slot]),
            device_id_type=MESH,
        )

    dkv_copies = {slot: dkv_copy(slot) for slot in range(1, 16)}

    def send_keys(group):
        for slot in range(4 * group + 3, 4 * group - 1, -1):
            if slot:
                dkv_out[slot, 0:DIM] = dk[slot].astype(BF16)
                dkv_out[slot, DIM:] = dv[slot].astype(BF16)
                dkv_copies[slot].start()

    def sib_copy(oz):
        return pltpu.make_async_remote_copy(
            src_ref=sib_out.at[oz],
            dst_ref=sib_in.at[oz],
            send_sem=sib_send.at[oz],
            recv_sem=sib_recv.at[oz],
            device_id=sibling,
            device_id_type=MESH,
        )

    sib_copies = [sib_copy(oz) for oz in range(NZ)]

    def dq_copy(oz):
        return pltpu.make_async_remote_copy(
            src_ref=dq_out.at[oz],
            dst_ref=dq_in.at[NZ - oz],
            send_sem=dq_send.at[oz],
            recv_sem=dq_recv.at[NZ - oz],
            device_id=along(oz),
            device_id_type=MESH,
        )

    dq_copies = {oz: dq_copy(oz) for oz in range(1, NZ)}

    def swap_queries(*offsets):
        for oz in offsets:
            sib_out[oz] = dq[own_slot(oz) + 1].astype(BF16)
            sib_copies[oz].start()

    def send_queries(*offsets):
        for oz in offsets:
            sib_copies[oz].wait_recv()
            total = dq[own_slot(oz)] + sib_in[oz].astype(F32)
            if oz:
                dq_out[oz] = total.astype(BF16)
                dq_copies[oz].start()
            else:
                dq[0] = total

    def relay(hop, chunk):
        for way in (1, -1):
            if (hop, chunk, way) in ring:
                ring[(hop, chunk, way)].wait_recv()
                for later in {1: (2,), 2: (3, 4)}.get(hop, ()):
                    if (later, chunk, way) in ring:
                        ring[(later, chunk, way)].start()
                pairs[(-way * hop % NZ, chunk)].start()

    def wait_pairs(*offsets):
        for oz in offsets:
            for chunk in range(2):
                pairs[(oz, chunk)].wait_recv()

    def before(step):
        if step == 0:
            relay(1, 0)
            relay(1, 1)
            wait_keys(0)
            relay_keys(0)
            wait_pairs(1, 7)
        if step == 1:
            wait_keys(1)
            relay_keys(1)
            relay(2, 0)
            pl.semaphore_wait(met.at[1], len(near))
            greet(2)
        if step == 2:
            relay(2, 1)
            wait_pairs(2, 6)
        if step == 4:
            wait_keys(2)
        if step == 5:
            pl.semaphore_wait(met.at[2], len(near))
            relay(3, 0)
        if step == 6:
            relay(3, 1)
            wait_keys(3)
        if step == 7:
            relay(4, 0)
            relay(4, 1)
        if step == 8:
            wait_pairs(3, 5)
        if step == 10:
            wait_pairs(0, 4)

    def after(step):
        if step == 6:
            swap_queries(1, 7)
        if step == 7:
            send_queries(1, 7)
            swap_queries(2, 6)
        if step == 8:
            send_queries(2, 6)
        if step == 10:
            send_keys(2)
        if step == 11:
            send_keys(3)
        if step == 13:
            swap_queries(3, 5)
        if step == 14:
            send_queries(3, 5)
            send_keys(1)
        if step == 15:
            swap_queries(4, 0)
            send_keys(0)
            send_queries(4, 0)

    def between(step):
        if step:
            after(step - 1)
        before(step)

    def tile(first_q, n_q, first_k, n_k):
        marks = ka[pl.ds(first_k, n_k)].reshape(n_k * ROWS, ROWS)
        k_part = kv[pl.ds(first_k, n_k), 0].reshape(n_k * ROWS, DIM)
        v_part = kv[pl.ds(first_k, n_k), 1].reshape(n_k * ROWS, DIM)
        k_wide = jnp.concatenate([k_part, marks], 1)
        v_wide = jnp.concatenate([v_part, marks], 1)
        q_cols = [
            jnp.concatenate([qd[first_q + a, head], qm[first_q + a]], 0)
            for a in range(n_q)
            for head in range(2)
        ]
        d_cols = [
            jnp.concatenate([qd[first_q + a, 2 + head], none], 0)
            for a in range(n_q)
            for head in range(2)
        ]
        q_wide = jnp.concatenate(q_cols, 1)
        d_wide = jnp.concatenate(d_cols, 1)
        scores = jnp.dot(k_wide, q_wide, preferred_element_type=F32)
        dprobs = jnp.dot(v_wide, d_wide, preferred_element_type=F32)
        probs = jnp.exp2(scores * EXP_SCALE)
        dscores = (probs * dprobs).astype(BF16)
        v_sum = lax.dot_general(
            probs.astype(BF16), d_wide[:DIM], NT, preferred_element_type=F32
        )
        k_sum = lax.dot_general(dscores, q_wide[:DIM], NT, preferred_element_type=F32)
        k_turned = jnp.concatenate([kt[first_k + a] for a in range(n_k)], 1)
        q_sum = jnp.dot(k_turned, dscores, preferred_element_type=F32)
        for a in range(n_k):
            dv[first_k + a] += v_sum[a * ROWS : (a + 1) * ROWS]
            dk[first_k + a] += k_sum[a * ROWS : (a + 1) * ROWS]
        for a in range(n_q):
            for head in range(2):
                col = (2 * a + head) * ROWS
                dq[first_q + a, pl.ds(head * DIM, DIM)] += q_sum[:, col : col + ROWS]

    tables = [
        [table(entry[part] for entry in TILES[8 * half : 8 * half + 8]) for part in range(3)]
        for half in range(2)
    ]

    def run_half(half, carry):
        lists = tuple(one + half * (two - one) for one, two in zip(*tables))

        def run_tile(at, lists):
            _, q_part, k_part = (one % 4 for one in lists)
            step = half * 8 + at
            for part in range(4):

                @pl.when(at // 2 == part)
                def _():
                    for n in (2 * part, 2 * part + 1, 2 * part + 8, 2 * part + 9):
                        pl.when(step == n)(functools.partial(between, n))

            tile(q_part * 4, 4, k_part * 4, 4)
            return tuple(one // 4 for one in lists)

        lax.fori_loop(0, 8, run_tile, lists)
        return carry

    lax.fori_loop(0, 2, run_half, 0)
    after(15)

    for oz in range(1, NZ):
        dq_copies[oz].wait_recv()
    total = dq[0]
    for oz in range(1, NZ):
        total = total + dq_in[oz].astype(F32)
    total = total * SCALE
    for head in range(2):
        part = total[head * DIM : (head + 1) * DIM]
        query_grad[:, pl.ds(head * DIM, DIM)] = part.T.astype(BF16)
    for slot in range(1, 16):
        dkv_copies[slot].wait_recv()
    k_total, v_total = dk[0], dv[0]
    for slot in range(1, 16):
        k_total = k_total + dkv_in[slot, 0:DIM].astype(F32)
        v_total = v_total + dkv_in[slot, DIM:].astype(F32)
    key_grad[...] = (k_total * SCALE).astype(BF16)
    value_grad[...] = v_total.astype(BF16)

    for copies in (kv_copies, kv_relays, dkv_copies, dq_copies, ring, pairs):
        for copy in copies.values():
            copy.wait_send()
    for copy in sib_copies:
        copy.wait_send()


def finish(q_in, k_in, v_in, q_out, k_out, v_out):
    q_out[...] = q_in[...]
    k_out[...] = k_in[...]
    v_out[...] = v_in[...]


def body(query, key, value, out_grad, attn_out, lse, positions):
    vmem = pl.BlockSpec(memory_space=pltpu.VMEM)
    dma = pltpu.SemaphoreType.DMA
    parts = pl.pallas_call(
        kernel,
        out_shape=(
            jax.ShapeDtypeStruct((ROWS, 2 * DIM), BF16),
            jax.ShapeDtypeStruct((ROWS, DIM), BF16),
            jax.ShapeDtypeStruct((ROWS, DIM), BF16),
        ),
        in_specs=[vmem] * 6 + [pl.BlockSpec(memory_space=pl.ANY)],
        out_specs=[vmem] * 3,
        scratch_shapes=[
            pltpu.VMEM((256, ROWS), jnp.int32),
            pltpu.VMEM((16, 4, DIM + AUG, ROWS), BF16),
            pltpu.VMEM((16, REST, ROWS), BF16),
            pltpu.VMEM((16, 2, ROWS, DIM), BF16),
            pltpu.VMEM((16, DIM, ROWS), BF16),
            pltpu.VMEM((16, ROWS, ROWS), BF16),
            pltpu.VMEM((32, ROWS), jnp.int32),
            pltpu.VMEM((16, 2 * DIM, ROWS), F32),
            pltpu.VMEM((16, DIM, ROWS), F32),
            pltpu.VMEM((16, DIM, ROWS), F32),
            pltpu.VMEM((8, 2 * DIM, ROWS), BF16),
            pltpu.VMEM((8, 2 * DIM, ROWS), BF16),
            pltpu.VMEM((8, 2 * DIM, ROWS), BF16),
            pltpu.VMEM((8, 2 * DIM, ROWS), BF16),
            pltpu.VMEM((16, 2 * DIM, ROWS), BF16),
            pltpu.VMEM((16, 2 * DIM, ROWS), BF16),
            dma,
            dma((16, 2)),
            dma((16, 2)),
            dma((2, 4, 2)),
            dma((16, 2)),
            dma((8, 2)),
            dma((8,)),
            dma((8,)),
            dma((8,)),
            dma((8,)),
            dma((16,)),
            dma((16,)),
            pltpu.SemaphoreType.REGULAR((3,)),
        ],
        compiler_params=pltpu.CompilerParams(
            collective_id=0, has_side_effects=True, vmem_limit_bytes=56 * 2**20
        ),
    )(query, key, value, out_grad, attn_out, lse.T, positions.reshape(256, ROWS))
    return pl.pallas_call(
        finish,
        out_shape=tuple(jax.ShapeDtypeStruct(part.shape, part.dtype) for part in parts),
        in_specs=[vmem] * 3,
        out_specs=[vmem] * 3,
    )(*parts)


def solution(mesh):
    split = P(("row", "col"), None)
    return jax.shard_map(
        body,
        mesh=mesh,
        in_specs=(split,) * 6 + (P(),),
        out_specs=(split,) * 3,
        check_vma=False,
    )
```

```python
import functools
import math

import jax
import jax.numpy as jnp
from jax import lax
from jax.experimental import pallas as pl
from jax.experimental.pallas import tpu as pltpu
from jax.sharding import PartitionSpec as P

F32 = jnp.float32
BF16 = jnp.bfloat16
MESH = pl.DeviceIdType.MESH
ROWS = 128
DIM = 128
NX, NY, NZ = 4, 4, 8
AUG = 16
REST = 112
SCALE = 1.0 / math.sqrt(DIM)
EXP_SCALE = math.log2(math.e) / math.sqrt(DIM)
FAR = -1e30
NT = (((1,), (1,)), ((), ()))

PAIRS = ((0, 4), (1, 7), (2, 6), (3, 5))
SPOT = {oz: 2 * group + at for group, pair in enumerate(PAIRS) for at, oz in enumerate(pair)}

KEY_SPOTS = (
    (0, 0), (1, 0), (3, 0), (2, 0), (0, 1), (0, 3), (0, 2), (1, 1),
    (3, 1), (1, 3), (2, 1), (1, 2), (3, 3), (2, 3), (3, 2), (2, 2),
)

TILES = (
    (0, 1, 0), (0, 1, 1), (0, 2, 0), (0, 2, 1), (0, 1, 2), (0, 2, 2), (0, 1, 3), (0, 2, 3),
    (0, 3, 2), (0, 3, 3), (0, 0, 2), (0, 0, 3), (0, 3, 1), (0, 3, 0), (0, 0, 1), (0, 0, 0),
)


def table(values):
    total = 0
    for at, value in enumerate(values):
        total += value * 4**at
    return total


def kernel(
    query, key, value, out_grad, attn_out, lse, positions,
    query_grad, key_grad, value_grad,
    pos, qd, qm, kv, kt, ka, kp, dq, dk, dv,
    sib_out, sib_in, dq_out, dq_in, dkv_out, dkv_in,
    pos_sem, kv_send, kv_recv, ring_send, q_recv, pair_send,
    sib_send, sib_recv, dq_send, dq_recv, dkv_send, dkv_recv, met,
):
    pos_copy = pltpu.make_async_copy(positions, pos, pos_sem)
    pos_copy.start()
    row, col = lax.axis_index("row"), lax.axis_index("col")
    core = lax.rem(col, 2)
    other = 1 - core
    x, z_lo = lax.div(col, 8), lax.rem(lax.div(col, 2), 4)
    y, z_hi = lax.div(row, 2), lax.rem(row, 2)
    z = z_hi * 4 + z_lo
    rows_y = [lax.rem(y + oy, NY) * 2 for oy in range(NY)]
    cols_x = [lax.rem(x + ox, NX) * 8 for ox in range(NX)]
    zs = [lax.rem(z + oz, NZ) for oz in range(NZ)]
    rows_z = [lax.div(one, 4) for one in zs]
    cols_z = [lax.rem(one, 4) * 2 for one in zs]

    def plane(ox, oy):
        return (rows_y[oy % NY] + z_hi, cols_x[ox % NX] + (z_lo * 2 + core))

    def along(oz, which=None):
        return (rows_y[0] + rows_z[oz % NZ], cols_x[0] + cols_z[oz % NZ] + (core if which is None else which))

    sibling = (row, col + 1 - 2 * core)

    barrier = pltpu.get_barrier_semaphore()
    near = [along(1), along(-1), plane(1, 0), plane(-1, 0), plane(0, 1), plane(0, -1), sibling]
    for peer in near:
        pl.semaphore_signal(barrier, inc=1, device_id=peer, device_id_type=MESH)

    def greet(turn):
        for peer in near:
            pl.semaphore_signal(met.at[turn], inc=1, device_id=peer, device_id_type=MESH)


    kv[0, 0] = key[...]
    kv[0, 1] = value[...]
    line = lax.broadcasted_iota(jnp.int32, (AUG, ROWS), 0)

    def split_rows(term):
        high = term.astype(BF16).astype(F32)
        rest = term - high
        middle = rest.astype(BF16).astype(F32)
        low = rest - middle
        picked = jnp.where(line == 0, high, jnp.where(line == 1, middle, low))
        return jnp.where(line < 3, picked, 0.0).astype(BF16)

    for head in range(2):
        cut = pl.ds(head * DIM, DIM)
        grads, outs = out_grad[:, cut], attn_out[:, cut]
        delta = jnp.sum((grads.astype(F32) * outs.astype(F32)).T, axis=0, keepdims=True)
        qd[0, head, 0:DIM] = query[:, cut].T
        qd[0, head, DIM : DIM + AUG] = split_rows(lse[head : head + 1, :] * -math.sqrt(DIM))
        qd[0, 2 + head, 0:DIM] = grads.T
        qd[0, 2 + head, DIM : DIM + AUG] = split_rows(-delta)

    pl.semaphore_wait(barrier, len(near))

    def own_slot(oz):
        return 2 * SPOT[oz % NZ]

    def ring_copy(hop, chunk, way):
        far = max(hop - 2, 1)
        source, target = own_slot(way * (far - hop)), own_slot(-way * hop)
        cut = pl.ds(2 * chunk, 2)
        return pltpu.make_async_remote_copy(
            src_ref=qd.at[source, cut],
            dst_ref=qd.at[target, cut],
            send_sem=ring_send.at[0 if way > 0 else 1, hop - 1, chunk],
            recv_sem=q_recv.at[target, chunk],
            device_id=along(way * far),
            device_id_type=MESH,
        )

    def pair_copy(oz, chunk):
        slot = own_slot(oz)
        cut = pl.ds(2 * chunk, 2)
        return pltpu.make_async_remote_copy(
            src_ref=qd.at[slot, cut],
            dst_ref=qd.at[slot + 1, cut],
            send_sem=pair_send.at[oz, chunk],
            recv_sem=q_recv.at[slot + 1, chunk],
            device_id=sibling,
            device_id_type=MESH,
        )

    ring = {
        (hop, chunk, way): ring_copy(hop, chunk, way)
        for hop in range(1, 5)
        for chunk in range(2)
        for way in (1, -1)
        if hop < 4 or (way > 0) == (chunk == 0)
    }
    pairs = {(oz, chunk): pair_copy(oz, chunk) for oz in range(NZ) for chunk in range(2)}

    def kv_copy(slot):
        ox, oy = KEY_SPOTS[slot]
        return pltpu.make_async_remote_copy(
            src_ref=kv.at[0],
            dst_ref=kv.at[slot],
            send_sem=kv_send.at[slot, 0],
            recv_sem=kv_recv.at[slot, 0],
            device_id=plane(-ox, -oy),
            device_id_type=MESH,
        )

    def kv_relay(slot, part):
        ox, oy = KEY_SPOTS[slot]
        middle = KEY_SPOTS.index((0, oy) if part else (ox, 0))
        return pltpu.make_async_remote_copy(
            src_ref=kv.at[middle, part],
            dst_ref=kv.at[slot, part],
            send_sem=kv_send.at[slot, part],
            recv_sem=kv_recv.at[slot, part],
            device_id=plane(-ox, 0) if part else plane(0, -oy),
            device_id_type=MESH,
        )

    kv_copies = {slot: kv_copy(slot) for slot in range(1, 8)}
    kv_relays = {(slot, part): kv_relay(slot, part) for slot in range(8, 16) for part in range(2)}

    def relay_keys(part):
        for slot in range(8, 16):
            kv_relays[(slot, part)].start()

    for chunk in range(2):
        for way in (1, -1):
            ring[(1, chunk, way)].start()
    for slot in (1, 2, 4, 5):
        kv_copies[slot].start()
    for chunk in range(2):
        pairs[(0, chunk)].start()
    greet(0)
    pos_copy.wait()

    dq[...] = jnp.zeros_like(dq)
    dk[...] = jnp.zeros_like(dk)
    dv[...] = jnp.zeros_like(dv)
    lane = lax.broadcasted_iota(jnp.int32, (ROWS, ROWS), 1)
    block = lax.broadcasted_iota(jnp.int32, (ROWS, ROWS), 0) // 64
    for slot in range(16):
        hot = (lane < 3) | (lane == AUG + 2 * slot + block)
        ka[slot] = jnp.where(hot, 1.0, 0.0).astype(BF16)
        r, c = plane(*KEY_SPOTS[slot])
        places = pos[pl.ds(r * 32 + c, 1), :] // 64
        kp[2 * slot : 2 * slot + 1, :] = jnp.broadcast_to(places[:, 0:1], (1, ROWS))
        kp[2 * slot + 1 : 2 * slot + 2, :] = jnp.broadcast_to(places[:, 64:65], (1, ROWS))
    for slot in range(16):
        r, c = along(PAIRS[slot // 4][slot // 2 % 2], other if slot % 2 else core)
        places = pos[pl.ds(r * 32 + c, 1), :] // 64
        bias = jnp.where(kp[...] < places, 0.0, FAR)
        qm[slot] = jnp.concatenate([bias, jnp.zeros((REST - 32, ROWS), F32)], 0).astype(BF16)

    pl.semaphore_wait(met.at[0], len(near))
    for slot in (3, 6, 7):
        kv_copies[slot].start()
    greet(1)

    def relay(hop, chunk):
        for way in (1, -1):
            if (hop, chunk, way) in ring:
                ring[(hop, chunk, way)].wait_recv()
                for later in {1: (2,), 2: (3, 4)}.get(hop, ()):
                    if (later, chunk, way) in ring:
                        ring[(later, chunk, way)].start()
                pairs[(-way * hop % NZ, chunk)].start()

    relay(1, 0)
    relay(1, 1)

    none = jnp.zeros((REST, ROWS), BF16)

    def turn(slot):
        kt[slot] = kv[slot, 0].T

    turn(0)
    keys = jnp.concatenate([kv[0, 0], ka[0]], 1)
    values = jnp.concatenate([kv[0, 1], ka[0]], 1)
    q_own = [qd[0, head] for head in range(4)]
    q_cat = jnp.concatenate([jnp.concatenate([part, none], 0) for part in q_own[:2]], 1)
    d_cat = jnp.concatenate([jnp.concatenate([part, none], 0) for part in q_own[2:]], 1)
    scores = jnp.dot(keys, q_cat, preferred_element_type=F32)
    dprobs = jnp.dot(values, d_cat, preferred_element_type=F32)
    at_key = lax.broadcasted_iota(jnp.int32, (ROWS, 2 * ROWS), 0)
    at_row = lax.broadcasted_iota(jnp.int32, (ROWS, 2 * ROWS), 1) % ROWS
    inside = (at_key <= at_row) & (at_key // 64 == at_row // 64)
    probs = jnp.where(inside, jnp.exp2(scores * EXP_SCALE), 0.0)
    dscores = (probs * dprobs).astype(BF16)
    dv[0] = lax.dot_general(probs.astype(BF16), d_cat[:DIM], NT, preferred_element_type=F32)
    dk[0] = lax.dot_general(dscores, q_cat[:DIM], NT, preferred_element_type=F32)
    part = jnp.dot(kt[0], dscores, preferred_element_type=F32)
    dq[0] = jnp.concatenate([part[:, :ROWS], part[:, ROWS:]], 0)

    def wait_keys(group):
        for slot in range(4 * group, 4 * group + 4):
            if slot in kv_copies:
                kv_copies[slot].wait_recv()
            if (slot, 0) in kv_relays:
                kv_relays[(slot, 0)].wait_recv()
                kv_relays[(slot, 1)].wait_recv()
            if slot:
                turn(slot)

    def dkv_copy(slot):
        return pltpu.make_async_remote_copy(
            src_ref=dkv_out.at[slot],
            dst_ref=dkv_in.at[slot],
            send_sem=dkv_send.at[slot],
            recv_sem=dkv_recv.at[slot],
            device_id=plane(*KEY_SPOTS[slot]),
            device_id_type=MESH,
        )

    dkv_copies = {slot: dkv_copy(slot) for slot in range(1, 16)}

    def send_keys(group):
        for slot in range(4 * group + 3, 4 * group - 1, -1):
            if slot:
                dkv_out[slot, 0:DIM] = dk[slot].astype(BF16)
                dkv_out[slot, DIM:] = dv[slot].astype(BF16)
                dkv_copies[slot].start()

    def sib_copy(oz):
        return pltpu.make_async_remote_copy(
            src_ref=sib_out.at[oz],
            dst_ref=sib_in.at[oz],
            send_sem=sib_send.at[oz],
            recv_sem=sib_recv.at[oz],
            device_id=sibling,
            device_id_type=MESH,
        )

    sib_copies = [sib_copy(oz) for oz in range(NZ)]

    def dq_copy(oz):
        return pltpu.make_async_remote_copy(
            src_ref=dq_out.at[oz],
            dst_ref=dq_in.at[NZ - oz],
            send_sem=dq_send.at[oz],
            recv_sem=dq_recv.at[NZ - oz],
            device_id=along(oz),
            device_id_type=MESH,
        )

    dq_copies = {oz: dq_copy(oz) for oz in range(1, NZ)}

    def swap_queries(*offsets):
        for oz in offsets:
            sib_out[oz] = dq[own_slot(oz) + 1].astype(BF16)
            sib_copies[oz].start()

    def send_queries(*offsets):
        for oz in offsets:
            sib_copies[oz].wait_recv()
            total = dq[own_slot(oz)] + sib_in[oz].astype(F32)
            if oz:
                dq_out[oz] = total.astype(BF16)
                dq_copies[oz].start()
            else:
                dq[0] = total

    def wait_pairs(*offsets):
        for oz in offsets:
            for chunk in range(2):
                pairs[(oz, chunk)].wait_recv()

    def before(step):
        if step == 0:
            wait_keys(0)
            relay_keys(0)
            wait_pairs(1, 7)
        if step == 1:
            wait_keys(1)
            relay_keys(1)
            relay(2, 0)
            pl.semaphore_wait(met.at[1], len(near))
            greet(2)
        if step == 2:
            relay(2, 1)
            wait_pairs(2, 6)
        if step == 4:
            wait_keys(2)
        if step == 5:
            pl.semaphore_wait(met.at[2], len(near))
            relay(3, 0)
        if step == 6:
            relay(3, 1)
            wait_keys(3)
        if step == 7:
            relay(4, 0)
            relay(4, 1)
        if step == 8:
            wait_pairs(3, 5)
        if step == 10:
            wait_pairs(0, 4)

    def after(step):
        if step == 6:
            swap_queries(1, 7)
        if step == 7:
            send_queries(1, 7)
            swap_queries(2, 6)
        if step == 8:
            send_queries(2, 6)
        if step == 10:
            send_keys(2)
        if step == 11:
            send_keys(3)
        if step == 13:
            swap_queries(3, 5)
        if step == 14:
            send_queries(3, 5)
            send_keys(1)
        if step == 15:
            swap_queries(4, 0)
            send_keys(0)
            send_queries(4, 0)

    def between(step):
        if step:
            after(step - 1)
        before(step)

    def tile(first_q, n_q, first_k, n_k):
        marks = ka[pl.ds(first_k, n_k)].reshape(n_k * ROWS, ROWS)
        k_part = kv[pl.ds(first_k, n_k), 0].reshape(n_k * ROWS, DIM)
        v_part = kv[pl.ds(first_k, n_k), 1].reshape(n_k * ROWS, DIM)
        k_wide = jnp.concatenate([k_part, marks], 1)
        v_wide = jnp.concatenate([v_part, marks], 1)
        q_cols = [
            jnp.concatenate([qd[first_q + a, head], qm[first_q + a]], 0)
            for a in range(n_q)
            for head in range(2)
        ]
        d_cols = [
            jnp.concatenate([qd[first_q + a, 2 + head], none], 0)
            for a in range(n_q)
            for head in range(2)
        ]
        q_wide = jnp.concatenate(q_cols, 1)
        d_wide = jnp.concatenate(d_cols, 1)
        scores = jnp.dot(k_wide, q_wide, preferred_element_type=F32)
        dprobs = jnp.dot(v_wide, d_wide, preferred_element_type=F32)
        probs = jnp.exp2(scores * EXP_SCALE)
        dscores = (probs * dprobs).astype(BF16)
        v_sum = lax.dot_general(
            probs.astype(BF16), d_wide[:DIM], NT, preferred_element_type=F32
        )
        k_sum = lax.dot_general(dscores, q_wide[:DIM], NT, preferred_element_type=F32)
        k_turned = jnp.concatenate([kt[first_k + a] for a in range(n_k)], 1)
        q_sum = jnp.dot(k_turned, dscores, preferred_element_type=F32)
        for a in range(n_k):
            dv[first_k + a] += v_sum[a * ROWS : (a + 1) * ROWS]
            dk[first_k + a] += k_sum[a * ROWS : (a + 1) * ROWS]
        for a in range(n_q):
            for head in range(2):
                col = (2 * a + head) * ROWS
                dq[first_q + a, pl.ds(head * DIM, DIM)] += q_sum[:, col : col + ROWS]

    tables = [
        [table(entry[part] for entry in TILES[8 * half : 8 * half + 8]) for part in range(3)]
        for half in range(2)
    ]

    def run_half(half, carry):
        lists = tuple(one + half * (two - one) for one, two in zip(*tables))

        def run_tile(at, lists):
            _, q_part, k_part = (one % 4 for one in lists)
            step = half * 8 + at
            for part in range(4):

                @pl.when(at // 2 == part)
                def _():
                    for n in (2 * part, 2 * part + 1, 2 * part + 8, 2 * part + 9):
                        pl.when(step == n)(functools.partial(between, n))

            tile(q_part * 4, 4, k_part * 4, 4)
            return tuple(one // 4 for one in lists)

        lax.fori_loop(0, 8, run_tile, lists)
        return carry

    lax.fori_loop(0, 2, run_half, 0)
    after(15)

    for oz in range(1, NZ):
        dq_copies[oz].wait_recv()
    total = dq[0]
    for oz in range(1, NZ):
        total = total + dq_in[oz].astype(F32)
    total = total * SCALE
    for head in range(2):
        part = total[head * DIM : (head + 1) * DIM]
        query_grad[:, pl.ds(head * DIM, DIM)] = part.T.astype(BF16)
    for slot in range(1, 16):
        dkv_copies[slot].wait_recv()
    k_total, v_total = dk[0], dv[0]
    for slot in range(1, 16):
        k_total = k_total + dkv_in[slot, 0:DIM].astype(F32)
        v_total = v_total + dkv_in[slot, DIM:].astype(F32)
    key_grad[...] = (k_total * SCALE).astype(BF16)
    value_grad[...] = v_total.astype(BF16)

    for copies in (kv_copies, kv_relays, dkv_copies, dq_copies, ring, pairs):
        for copy in copies.values():
            copy.wait_send()
    for copy in sib_copies:
        copy.wait_send()


def finish(q_in, k_in, v_in, q_out, k_out, v_out):
    q_out[...] = q_in[...]
    k_out[...] = k_in[...]
    v_out[...] = v_in[...]


def body(query, key, value, out_grad, attn_out, lse, positions):
    vmem = pl.BlockSpec(memory_space=pltpu.VMEM)
    dma = pltpu.SemaphoreType.DMA
    parts = pl.pallas_call(
        kernel,
        out_shape=(
            jax.ShapeDtypeStruct((ROWS, 2 * DIM), BF16),
            jax.ShapeDtypeStruct((ROWS, DIM), BF16),
            jax.ShapeDtypeStruct((ROWS, DIM), BF16),
        ),
        in_specs=[vmem] * 6 + [pl.BlockSpec(memory_space=pl.ANY)],
        out_specs=[vmem] * 3,
        scratch_shapes=[
            pltpu.VMEM((256, ROWS), jnp.int32),
            pltpu.VMEM((16, 4, DIM + AUG, ROWS), BF16),
            pltpu.VMEM((16, REST, ROWS), BF16),
            pltpu.VMEM((16, 2, ROWS, DIM), BF16),
            pltpu.VMEM((16, DIM, ROWS), BF16),
            pltpu.VMEM((16, ROWS, ROWS), BF16),
            pltpu.VMEM((32, ROWS), jnp.int32),
            pltpu.VMEM((16, 2 * DIM, ROWS), F32),
            pltpu.VMEM((16, DIM, ROWS), F32),
            pltpu.VMEM((16, DIM, ROWS), F32),
            pltpu.VMEM((8, 2 * DIM, ROWS), BF16),
            pltpu.VMEM((8, 2 * DIM, ROWS), BF16),
            pltpu.VMEM((8, 2 * DIM, ROWS), BF16),
            pltpu.VMEM((8, 2 * DIM, ROWS), BF16),
            pltpu.VMEM((16, 2 * DIM, ROWS), BF16),
            pltpu.VMEM((16, 2 * DIM, ROWS), BF16),
            dma,
            dma((16, 2)),
            dma((16, 2)),
            dma((2, 4, 2)),
            dma((16, 2)),
            dma((8, 2)),
            dma((8,)),
            dma((8,)),
            dma((8,)),
            dma((8,)),
            dma((16,)),
            dma((16,)),
            pltpu.SemaphoreType.REGULAR((3,)),
        ],
        compiler_params=pltpu.CompilerParams(
            collective_id=0, has_side_effects=True, vmem_limit_bytes=56 * 2**20
        ),
    )(query, key, value, out_grad, attn_out, lse.T, positions.reshape(256, ROWS))
    return pl.pallas_call(
        finish,
        out_shape=tuple(jax.ShapeDtypeStruct(part.shape, part.dtype) for part in parts),
        in_specs=[vmem] * 3,
        out_specs=[vmem] * 3,
    )(*parts)


def solution(mesh):
    split = P(("row", "col"), None)
    return jax.shard_map(
        body,
        mesh=mesh,
        in_specs=(split,) * 6 + (P(),),
        out_specs=(split,) * 3,
        check_vma=False,
    )
```
